32 devices in a mesh: ty: 4 (over z), tx: 8 (over y, x, core).
Axes of the slice: x: 2, y: 2, z: 4, core: 2. Of those that a mesh axis runs over, the one named last changes fastest.
Arguments:
- track_rows: float32 [16384, 2, 256], P(('ty', 'tx')), may hold values from -6 to 6
- track_tile: int32 [16384, 1], P(('ty', 'tx')), may hold values from 0 to 31; in each aligned block of 512 rows (0 to 511, 512 to 1023, ...) at most 32 rows name the same one
- track_slot: int32 [16384], P(('ty', 'tx')), may hold values from 0 to 2047
- velocity: float32 [2, 1024, 16384], P(None, 'ty', 'tx'), may hold values from -6 to 6
- viscosity: float32 [1024, 16384], P('ty', 'tx'), may hold values from 0.5 to 2
- log_friction: float32 [1024, 16384], P('ty', 'tx'), may hold values from -0.7 to 1.6
Outputs:
- adjoint: float32 [2, 1024, 16384], P(None, 'ty', 'tx')
- grad_slab: float32 [64, 1024], P(('ty', 'tx'))
The draws below stay inside these ranges and needn't reach their ends.
Inputs may be any that keep to these rules, and one draw needn't show every extreme that they name: `track_tile`: among the 512 rows of one device at most 32 name the same tile, a bound that some block reaches.
All inputs are finite; a program needn't handle non-finite values.
Results may differ from the reference program's by a relative error of at most 0.00002.
Values sent between devices are 32-bit elements; how exact they have to be, the bound alone decides.
A program may use at most 128 MiB of HBM per device.

```python
import math
import jax
import jax.numpy as jnp
import numpy as np

CY = 256
CX = 2048
ROWS_DEV = 512
SEG = 256
CB = 16
SWEEPS = 3
NY = 1024
NX = 16384
ROWS = 16384
CAP = 32
SLOTS = 2048
DEVICES = 32


def place_ends(result, own_key, low, largest):
    longest = result.shape.index(max(result.shape))
    spots = []
    for shift in (0, 1):
        where = [jax.random.randint(jax.random.fold_in(own_key, axis), (), 0, length) for axis, length in enumerate(result.shape)]
        where[longest] = (where[longest] + shift) % result.shape[longest]
        spots.append(tuple(where))
    return result.at[spots[0]].set(low).at[spots[1]].set(largest)


def block_scale(own_key, shape, shards, smallest, largest):
    def one(axis_at, parts):
        heights = jax.random.uniform(jax.random.fold_in(jax.random.fold_in(own_key, 6), axis_at), (parts,), jnp.float32, smallest / len(shards), largest / len(shards))
        return jnp.repeat(jnp.exp(heights), shape[axis_at] // parts).reshape((-1,) + (1,) * (len(shape) - axis_at - 1))

    loudness = one(*shards[0])
    for cut in shards[1:]:
        loudness = loudness * one(*cut)
    return loudness


def deal_out(stream_key, own, number, rows, count, top, bound, lean):
    order = jax.random.permutation(stream_key, count)
    packed, ordinary = load_shares(count, rows * top, bound, lean, True), load_shares(count, rows * top, bound, lean, False)
    places = jnp.arange(count)

    def named(tallies, turn):
        used = int((tallies > 0).sum())
        fixed = max(1, used // 4)
        moved = fixed + (places - fixed + turn * (used - fixed)) % max(1, count - fixed)
        return jnp.zeros((count,), jnp.int32).at[order[jnp.where(places < fixed, places, moved)]].set(jnp.asarray(tallies, jnp.int32))

    tallies = jnp.where(number % 4 == 0, named(packed, number // 4), named(ordinary, number - number // 4 - 1))
    mixed = jax.random.permutation(jax.random.fold_in(own, 3), count)
    giver, receiver = mixed[0:count // 2 * 2:2], mixed[1:count // 2 * 2:2]
    slack = jnp.minimum(tallies[giver] - 1, bound - tallies[receiver]) // 2
    slack = jnp.where((giver == order[0]) | (receiver == order[0]) | (tallies[receiver] == 0), 0, jnp.maximum(slack, 0))
    moved = jax.random.randint(jax.random.fold_in(own, 4), (count // 2,), 0, 1 << 20) % (slack + 1)
    tallies = tallies.at[giver].add(-moved).at[receiver].add(moved)
    items = jnp.searchsorted(jnp.cumsum(tallies), jnp.arange(rows * top), side="right").astype(jnp.int32)
    listing = items.reshape(top, rows).T
    listing = listing[jax.random.permutation(jax.random.fold_in(own, 1), rows)]
    turn = jax.random.randint(jax.random.fold_in(own, 2), (rows, 1), 0, top)
    return jnp.take_along_axis(listing, (jnp.arange(top)[None, :] + turn) % top, axis=1)


def load_shares(amount, total, limit, slope, full):
    loads = [(1 << 20) // math.isqrt(rank ** slope) + 1 for rank in range(1, amount + 1)]
    largest = limit if full else min(limit, max(-(-total // amount), total * loads[0] // sum(loads)))
    least = 1 if total - largest >= amount - 1 else 0
    given, rest = [largest] + [least] * (amount - 1), total - largest - least * (amount - 1)
    while rest > 0:
        movable = [i for i in range(1, amount) if given[i] < largest] or [i for i in range(1, amount) if given[i] < limit]
        whole, remaining = sum([loads[i] for i in movable]), rest
        for i in movable:
            extra = min(limit - given[i], max(1, remaining * loads[i] // whole), rest)
            given[i] = given[i] + extra
            rest = rest - extra
    return np.array(given)


def gaussian(stream_key, dims, scale, reach, split=(), held_as=jnp.bfloat16):
    gain = block_scale(stream_key, dims, split, -0.22, 0.18) if split else 1.0
    entries = jax.random.normal(stream_key, dims, jnp.float32) * scale * gain
    return jnp.minimum(jnp.maximum(entries, -reach), reach).astype(held_as)


def setup_inputs(seed: int = 0) -> dict:
    arg_keys = jax.random.split(jax.random.key(seed), 7)
    track_rows = gaussian(arg_keys[0], (ROWS, 2, SEG), 1.0, 6.0, ((0, 32),), jnp.float32)
    track_tile_keys = jax.random.split(jax.random.fold_in(arg_keys[1], 1), ROWS // ROWS_DEV)
    track_tile_turns = jax.random.permutation(jax.random.fold_in(arg_keys[1], 3), ROWS // ROWS_DEV)
    track_tile = jax.vmap(lambda own, number: deal_out(jax.random.fold_in(arg_keys[1], 2), own, number, ROWS_DEV, DEVICES, 1, CAP, 2))(track_tile_keys, track_tile_turns).reshape((ROWS, 1))
    track_slot = place_ends(jax.random.randint(arg_keys[2], (ROWS,), 0, SLOTS), jax.random.fold_in(arg_keys[2], 1), 0, SLOTS - 1).astype(jnp.int32)
    velocity = gaussian(arg_keys[3], (2, NY, NX), 1.0, 6.0, ((1, 4), (2, 8)), jnp.float32)
    viscosity = jnp.clip(jnp.exp(math.log(2.0) - 1.3862944 * jax.random.uniform(arg_keys[4], (NY, NX), jnp.float32) ** block_scale(arg_keys[4], (NY, NX), ((0, 4), (1, 8)), -0.2, 0.2)), 0.5, 2.0)
    log_friction = jnp.clip(-0.7 + 2.3 * jax.random.uniform(arg_keys[5], (NY, NX), jnp.float32) ** block_scale(arg_keys[5], (NY, NX), ((0, 4), (1, 8)), -0.2, 0.2), -0.7, 1.6)
    return {"track_rows": track_rows, "track_tile": track_tile, "track_slot": track_slot, "velocity": velocity, "viscosity": viscosity, "log_friction": log_friction}


OMEGA = 0.8
CROSS_COUPLING = 3.0
REGULAR = 0.1


def face_terms(eta_pad):
    central_stencil = eta_pad[1:-1, 1:-1]
    eastern_neighbor = 0.5 * (central_stencil + eta_pad[1:-1, 2:])
    western_neighbor = 0.5 * (central_stencil + eta_pad[1:-1, :-2])
    northern_neighbor = 0.5 * (central_stencil + eta_pad[2:, 1:-1])
    southern_neighbor = 0.5 * (central_stencil + eta_pad[:-2, 1:-1])
    return central_stencil, eastern_neighbor, western_neighbor, northern_neighbor, southern_neighbor


def diagonal(eta_pad, friction_coeff):
    central_stencil, eastern_neighbor, western_neighbor, northern_neighbor, southern_neighbor = face_terms(eta_pad)
    diag_u = 4.0 * (eastern_neighbor + western_neighbor) + northern_neighbor + southern_neighbor + friction_coeff
    diag_v = 4.0 * (northern_neighbor + southern_neighbor) + eastern_neighbor + western_neighbor + friction_coeff
    return jnp.stack([diag_u, diag_v])


def mixed_derivative(field):
    return 0.25 * (field[2:, 2:] - field[2:, :-2] - field[:-2, 2:] + field[:-2, :-2])


def relax(multiplier_padded, force, eta_pad, friction_coeff):
    central_stencil, eastern_neighbor, western_neighbor, northern_neighbor, southern_neighbor = face_terms(eta_pad)
    u_padded_field = multiplier_padded[0]
    v_padded_field = multiplier_padded[1]
    u_interior = u_padded_field[1:-1, 1:-1]
    v_interior = v_padded_field[1:-1, 1:-1]
    apply_operator_u = 4.0 * (eastern_neighbor * (u_interior - u_padded_field[1:-1, 2:]) + western_neighbor * (u_interior - u_padded_field[1:-1, :-2])) + northern_neighbor * (u_interior - u_padded_field[2:, 1:-1]) + southern_neighbor * (u_interior - u_padded_field[:-2, 1:-1]) - CROSS_COUPLING * central_stencil * mixed_derivative(v_padded_field) + friction_coeff * u_interior
    apply_operator_v = 4.0 * (northern_neighbor * (v_interior - v_padded_field[2:, 1:-1]) + southern_neighbor * (v_interior - v_padded_field[:-2, 1:-1])) + eastern_neighbor * (v_interior - v_padded_field[1:-1, 2:]) + western_neighbor * (v_interior - v_padded_field[1:-1, :-2]) - CROSS_COUPLING * central_stencil * mixed_derivative(u_padded_field) + friction_coeff * v_interior
    return jnp.stack([u_interior, v_interior]) + OMEGA * (force - jnp.stack([apply_operator_u, apply_operator_v])) / diagonal(eta_pad, friction_coeff)


def smoothing(q_pad):
    q_mid = q_pad[1:-1, 1:-1]
    return 4.0 * q_mid - (((q_pad[1:-1, 2:] + q_pad[1:-1, :-2]) + q_pad[2:, 1:-1]) + q_pad[:-2, 1:-1])


def reference(track_rows, track_tile, track_slot, velocity, viscosity, log_friction):
    rows_all, cols_all = viscosity.shape
    segs = CX // SEG
    tiles_x = cols_all // CX
    tile = track_tile[:, 0]
    tile_y = tile // tiles_x
    tile_x = tile % tiles_x
    grid_row = tile_y * CY + track_slot // segs
    grid_seg = tile_x * segs + track_slot % segs
    target = (grid_row * (cols_all // SEG) + grid_seg).astype(jnp.int32)
    forcing = jax.ops.segment_sum(track_rows, target, num_segments=rows_all * cols_all // SEG)
    forcing = forcing.reshape(rows_all, cols_all // SEG, 2, SEG).transpose(2, 0, 1, 3).reshape(2, rows_all, cols_all)
    friction_coeff = jnp.exp(log_friction)
    eta_pad = jnp.pad(viscosity, 1)
    adjoint = OMEGA * forcing / diagonal(eta_pad, friction_coeff)
    for sweep in range(SWEEPS - 1):
        adjoint = relax(jnp.pad(adjoint, ((0, 0), (1, 1), (1, 1))), forcing, eta_pad, friction_coeff)
    gradient = -friction_coeff * (velocity[0] * adjoint[0] + velocity[1] * adjoint[1]) + REGULAR * smoothing(jnp.pad(log_friction, 1))
    grad_slab = gradient.reshape(rows_all // CB, CB, cols_all // CB, CB).sum(axis=(1, 3))
    return adjoint, grad_slab
```

```python
import functools

import jax
import jax.numpy as jnp
from jax import lax
from jax.experimental import pallas as pl
from jax.experimental.pallas import tpu as pltpu
from jax.sharding import PartitionSpec as P

CB = 16
OMEGA = 0.8
REGULAR = 0.1
RH = 8
CH = 128
R0 = 16
VMEM_LIMIT = 56 * 1024 * 1024


def pack_kernel(cap, tile_ref, slot_ref, rows_ref, out_ref, count):
    devices = out_ref.shape[0]
    lanes = lax.broadcasted_iota(jnp.int32, (4, 128), 1)

    def clear(d, carry):
        count[d] = 0
        out_ref[d, cap] = jnp.zeros((4, 128), jnp.float32)
        return carry

    lax.fori_loop(0, devices, clear, 0)

    def place(i, carry):
        t = tile_ref[i]
        r = count[t]
        count[t] = r + 1
        out_ref[t, r] = rows_ref[i]
        slot = slot_ref[i].astype(jnp.float32)
        filled = (r + 1).astype(jnp.float32)
        head = out_ref[t, cap]
        out_ref[t, cap] = jnp.where(lanes == r, slot, jnp.where(lanes == cap, filled, head))
        return carry

    lax.fori_loop(0, rows_ref.shape[0], place, 0)


def scatter_kernel(cap, segs, meta_ref, got_ref, out_ref):
    out_ref[...] = jnp.zeros_like(out_ref)
    lanes = lax.broadcasted_iota(jnp.int32, (8, 128), 0)

    def source(s, carry):
        def add(r, inner):
            slot = meta_ref[s * 128 + r]
            y = slot // segs
            x = pl.multiple_of((slot % segs) * 256, 256)
            base = pl.multiple_of(y // 8 * 8, 8)
            chosen = lanes == y % 8
            spots = [(c, pl.ds(base, 8), pl.ds(x + 128 * h, 128)) for h in range(2) for c in range(2)]
            olds = [out_ref[spot] for spot in spots]
            news = [got_ref[s, r, pl.ds(j, 1), :] for j in range(4)]
            for spot, old, new in zip(spots, olds, news):
                out_ref[spot] = old + jnp.where(chosen, new, 0.0)
            return inner

        return lax.fori_loop(0, meta_ref[s * 128 + cap], add, carry)

    lax.fori_loop(0, got_ref.shape[0], source, 0)


def stencil_kernel(
    f_in, ft, fb, fl, fr, eta_in, q_in, et, eb, el, er, vel_in,
    adj_out, coarse_out,
    f, eta, q, a0, a1, inv, vel, gsum, sems,
):
    _, rows, cols = f_in.shape
    width = cols + 2 * CH
    ty, tx = lax.axis_index("ty"), lax.axis_index("tx")
    mid = (pl.ds(R0, rows), pl.ds(CH, cols))
    top = (pl.ds(R0 - RH, RH), pl.ds(CH, cols))
    bottom = (pl.ds(R0 + rows, RH), pl.ds(CH, cols))
    left = (pl.ds(R0 - RH, rows + 2 * RH), pl.ds(0, CH))
    right = (pl.ds(R0 - RH, rows + 2 * RH), pl.ds(CH + cols, CH))
    moves = []
    for i, (core, field) in enumerate(((eta_in, eta), (q_in, q))):
        moves.append((core, field.at[mid]))
        for edge, spot in ((et, top), (eb, bottom), (el, left), (er, right)):
            moves.append((edge.at[i], field.at[spot]))
    n_first = len(moves)
    for c in range(2):
        moves.append((f_in.at[c], f.at[(c,) + mid]))
        for edge, spot in ((ft, top), (fb, bottom), (fl, left), (fr, right)):
            moves.append((edge.at[c], f.at[(c,) + spot]))
    n_second = len(moves)
    moves.append((vel_in, vel))
    copies = [pltpu.make_async_copy(a, b, sems.at[i]) for i, (a, b) in enumerate(moves)]
    for copy in copies:
        copy.start()
    for copy in copies[:n_second]:
        copy.wait()

    def window(ref, start, *lead):
        return ref[lead + (pl.ds(start - 8, 24), slice(None))]

    def shifts(w):
        return w[9:17], w[7:15]

    def to_left(x):
        return pltpu.roll(x, width - 1, 1)

    def to_right(x):
        return pltpu.roll(x, 1, 1)

    def prepare(k, carry):
        start = pl.multiple_of(8 * k, 8)
        here = pl.ds(start, 8)
        w = window(eta, start)
        mine = w[8:16]
        nxt, prv = shifts(w)
        y_sum = nxt + prv
        x_sum = to_left(mine) + to_right(mine)
        base = 5.0 * mine + jnp.exp(q[here, :])
        inv_u = OMEGA / (base + 2.0 * x_sum + 0.5 * y_sum)
        inv_v = OMEGA / (base + 2.0 * y_sum + 0.5 * x_sum)
        inv[0, here, :] = inv_u
        inv[1, here, :] = inv_v
        a0[0, here, :] = inv_u * f[0, here, :]
        a0[1, here, :] = inv_v * f[1, here, :]
        return carry

    chunks = (rows + 2 * RH) // 8
    lax.fori_loop(1, 1 + chunks, prepare, 0)

    def sweep(src, start):
        here = pl.ds(start, 8)
        e = window(eta, start)
        u, v = window(src, start, 0), window(src, start, 1)
        gu, gv = e * u, e * v
        em, um, vm = e[8:16], u[8:16], v[8:16]
        gum, gvm = gu[8:16], gv[8:16]
        un, us = shifts(u)
        vn, vs = shifts(v)
        gun, gus = shifts(gu)
        gvn, gvs = shifts(gv)
        du, dv = 0.75 * (un - us), 0.75 * (vn - vs)
        u2, v2 = 2.0 * um, 0.5 * vm
        su = f[0, here, :] + em * (to_left(u2 + dv) + to_right(u2 - dv) + 0.5 * (un + us))
        su = su + 2.0 * (to_left(gum) + to_right(gum)) + 0.5 * (gun + gus)
        sv = f[1, here, :] + em * (to_left(v2 + du) + to_right(v2 - du) + 2.0 * (vn + vs))
        sv = sv + 0.5 * (to_left(gvm) + to_right(gvm)) + 2.0 * (gvn + gvs)
        keep = 1.0 - OMEGA
        return keep * um + inv[0, here, :] * su, keep * vm + inv[1, here, :] * sv

    def second(k, carry):
        start = pl.multiple_of(8 * k, 8)
        u, v = sweep(a0, start)
        a1[0, pl.ds(start, 8), :] = u
        a1[1, pl.ds(start, 8), :] = v
        return carry

    lax.fori_loop(1, 1 + chunks, second, 0)

    @pl.when(ty == 0)
    def _():
        a1[:, R0 - RH : R0, :] = jnp.zeros((2, RH, width), jnp.float32)

    @pl.when(ty == lax.axis_size("ty") - 1)
    def _():
        a1[:, R0 + rows : R0 + rows + RH, :] = jnp.zeros((2, RH, width), jnp.float32)

    @pl.when(tx == 0)
    def _():
        a1[:, :, :CH] = jnp.zeros((2, a1.shape[1], CH), jnp.float32)

    @pl.when(tx == lax.axis_size("tx") - 1)
    def _():
        a1[:, :, CH + cols :] = jnp.zeros((2, a1.shape[1], CH), jnp.float32)

    copies[-1].wait()
    inner = slice(CH, CH + cols)

    def third(k, carry):
        total = jnp.zeros((8, cols), jnp.float32)
        for half in range(CB // 8):
            own = pl.multiple_of(CB * k + 8 * half, 8)
            start = pl.multiple_of(own + R0, 8)
            u, v = sweep(a1, start)
            u, v = u[:, inner], v[:, inner]
            adj_out[0, pl.ds(own, 8), :] = u
            adj_out[1, pl.ds(own, 8), :] = v
            w = window(q, start)
            nxt, prv = shifts(w)
            mine = w[8:16]
            smooth = (4.0 * mine - (to_left(mine) + to_right(mine) + nxt + prv))[:, inner]
            data = vel[0, pl.ds(own, 8), :] * u + vel[1, pl.ds(own, 8), :] * v
            total = total + REGULAR * smooth - jnp.exp(mine[:, inner]) * data
        gsum[pl.ds(pl.multiple_of(8 * k, 8), 8), :] = total
        return carry

    lax.fori_loop(0, rows // CB, third, 0)
    sums = jnp.sum(gsum[...].reshape(rows // CB, 8, cols), axis=1)
    cell = lax.broadcasted_iota(jnp.int32, (cols, cols // CB), 0) // CB
    column = lax.broadcasted_iota(jnp.int32, (cols, cols // CB), 1)
    pick = (cell == column).astype(jnp.float32)
    coarse = jnp.dot(
        sums, pick, preferred_element_type=jnp.float32, precision=lax.Precision.HIGHEST
    )
    share = coarse_out.shape[1]
    for i in range(coarse_out.shape[0]):
        coarse_out[i] = coarse[i * share : (i + 1) * share]


def halos(x):
    rows, cols = x.shape[1:]

    def both(axis, last, first):
        up = [(i, i + 1) for i in range(lax.axis_size(axis) - 1)]
        down = [(j, i) for i, j in up]
        return lax.ppermute(last, axis, up), lax.ppermute(first, axis, down)

    top, bottom = both("ty", x[:, rows - RH :], x[:, :RH])

    def side(part):
        return jnp.concatenate([top[:, :, part], x[:, :, part], bottom[:, :, part]], axis=1)

    left, right = both("tx", side(slice(cols - CH, cols)), side(slice(0, CH)))
    return top, bottom, left, right


VMEM = pl.BlockSpec(memory_space=pltpu.VMEM)
SMEM = pl.BlockSpec(memory_space=pltpu.SMEM)
ANY = pl.BlockSpec(memory_space=pl.ANY)


def shards(track_rows, track_tile, track_slot, velocity, viscosity, log_friction):
    rows, cols = viscosity.shape
    tiles_x = lax.axis_size("tx")
    devices = lax.axis_size("ty") * tiles_x
    rows_dev, _, seg = track_rows.shape
    cap = max(2, 2 * rows_dev // devices)
    params = pltpu.CompilerParams(vmem_limit_bytes=VMEM_LIMIT)
    f32 = jnp.float32
    block = track_rows.reshape(rows_dev, 2, 2, 128).transpose(0, 2, 1, 3).reshape(rows_dev, 4, 128)
    packed = pl.pallas_call(
        functools.partial(pack_kernel, cap),
        out_shape=jax.ShapeDtypeStruct((devices, cap + 1, 4, 128), f32),
        in_specs=[SMEM, SMEM, VMEM],
        out_specs=VMEM,
        scratch_shapes=[pltpu.SMEM((devices,), jnp.int32)],
        compiler_params=params,
        name="pack",
    )(track_tile[:, 0], track_slot, block)
    got = lax.all_to_all(packed, ("ty", "tx"), split_axis=0, concat_axis=0, tiled=True)
    eq_halo = halos(jnp.stack([viscosity, log_friction]))
    meta = got[:, cap, 0, :].astype(jnp.int32).reshape(devices * 128)
    forcing = pl.pallas_call(
        functools.partial(scatter_kernel, cap, cols // seg),
        out_shape=jax.ShapeDtypeStruct((2, rows, cols), f32),
        in_specs=[SMEM, VMEM],
        out_specs=VMEM,
        compiler_params=params,
        name="scatter",
    )(meta, got)
    f_halo = halos(forcing)
    coarse_rows = rows // CB
    big = (rows + 2 * R0, cols + 2 * CH)
    adjoint, coarse = pl.pallas_call(
        stencil_kernel,
        out_shape=(
            jax.ShapeDtypeStruct((2, rows, cols), f32),
            jax.ShapeDtypeStruct((tiles_x, coarse_rows // tiles_x, cols // CB), f32),
        ),
        in_specs=[ANY] * 12,
        out_specs=(VMEM, VMEM),
        scratch_shapes=[
            pltpu.VMEM((2,) + big, f32),
            pltpu.VMEM(big, f32),
            pltpu.VMEM(big, f32),
            pltpu.VMEM((2,) + big, f32),
            pltpu.VMEM((2,) + big, f32),
            pltpu.VMEM((2,) + big, f32),
            pltpu.VMEM((2, rows, cols), f32),
            pltpu.VMEM((coarse_rows * 8, cols), f32),
            pltpu.SemaphoreType.DMA((21,)),
        ],
        compiler_params=params,
        name="stencil",
    )(forcing, *f_halo, viscosity, log_friction, *eq_halo, velocity)
    grad = lax.all_to_all(coarse, "tx", split_axis=0, concat_axis=2, tiled=True)
    return adjoint, grad[0]


def solution(mesh):
    return jax.shard_map(
        shards,
        mesh=mesh,
        in_specs=(
            P(("ty", "tx"), None, None),
            P(("ty", "tx"), None),
            P(("ty", "tx")),
            P(None, "ty", "tx"),
            P("ty", "tx"),
            P("ty", "tx"),
        ),
        out_specs=(P(None, "ty", "tx"), P(("ty", "tx"), None)),
        check_vma=False,
    )
```

```python
import functools

import jax
import jax.numpy as jnp
from jax import lax
from jax.experimental import pallas as pl
from jax.experimental.pallas import tpu as pltpu
from jax.sharding import PartitionSpec as P

CB = 16
OMEGA = 0.8
REGULAR = 0.1
RH = 8
CH = 128
R0 = 16
VMEM_LIMIT = 56 * 1024 * 1024


def pack_kernel(cap, tile_ref, slot_ref, rows_ref, out_ref, count):
    devices = out_ref.shape[0]
    lanes = lax.broadcasted_iota(jnp.int32, (4, 128), 1)

    def clear(d, carry):
        count[d] = 0
        out_ref[d, cap] = jnp.zeros((4, 128), jnp.float32)
        return carry

    lax.fori_loop(0, devices, clear, 0)

    def place(i, carry):
        t = tile_ref[i]
        r = count[t]
        count[t] = r + 1
        out_ref[t, r] = rows_ref[i]
        slot = slot_ref[i].astype(jnp.float32)
        filled = (r + 1).astype(jnp.float32)
        head = out_ref[t, cap]
        out_ref[t, cap] = jnp.where(lanes == r, slot, jnp.where(lanes == cap, filled, head))
        return carry

    lax.fori_loop(0, rows_ref.shape[0], place, 0)


def scatter_kernel(cap, segs, meta_ref, got_ref, out_ref):
    out_ref[...] = jnp.zeros_like(out_ref)
    lanes = lax.broadcasted_iota(jnp.int32, (8, 128), 0)

    def source(s, carry):
        def add(r, inner):
            slot = meta_ref[s * 128 + r]
            y = slot // segs
            x = pl.multiple_of((slot % segs) * 256, 256)
            base = pl.multiple_of(y // 8 * 8, 8)
            chosen = lanes == y % 8
            spots = [(c, pl.ds(base, 8), pl.ds(x + 128 * h, 128)) for h in range(2) for c in range(2)]
            olds = [out_ref[spot] for spot in spots]
            news = [got_ref[s, r, pl.ds(j, 1), :] for j in range(4)]
            for spot, old, new in zip(spots, olds, news):
                out_ref[spot] = old + jnp.where(chosen, new, 0.0)
            return inner

        return lax.fori_loop(0, meta_ref[s * 128 + cap], add, carry)

    lax.fori_loop(0, got_ref.shape[0], source, 0)


def stencil_kernel(
    f_in, ft, fb, fl, fr, eta_in, q_in, et, eb, el, er, qt, qb, ql, qr, vel_in,
    adj_out, coarse_out,
    f, eta, q, a0, a1, inv, vel, gsum, sems,
):
    _, rows, cols = f_in.shape
    width = cols + 2 * CH
    ty, tx = lax.axis_index("ty"), lax.axis_index("tx")
    mid = (pl.ds(R0, rows), pl.ds(CH, cols))
    top = (pl.ds(R0 - RH, RH), pl.ds(CH, cols))
    bottom = (pl.ds(R0 + rows, RH), pl.ds(CH, cols))
    left = (pl.ds(R0 - RH, rows + 2 * RH), pl.ds(0, CH))
    right = (pl.ds(R0 - RH, rows + 2 * RH), pl.ds(CH + cols, CH))
    moves = []
    for field, *parts in ((eta, eta_in, et, eb, el, er), (q, q_in, qt, qb, ql, qr)):
        for part, spot in zip(parts, (mid, top, bottom, left, right)):
            moves.append((part, field.at[spot]))
    for c in range(2):
        moves.append((f_in.at[c], f.at[(c,) + mid]))
        for edge, spot in ((ft, top), (fb, bottom), (fl, left), (fr, right)):
            moves.append((edge.at[c], f.at[(c,) + spot]))
    n_second = len(moves)
    moves.append((vel_in, vel))
    copies = [pltpu.make_async_copy(a, b, sems.at[i]) for i, (a, b) in enumerate(moves)]
    for copy in copies:
        copy.start()
    for copy in copies[:n_second]:
        copy.wait()

    def window(ref, start, *lead):
        return ref[lead + (pl.ds(start - 8, 24), slice(None))]

    def shifts(w):
        return w[9:17], w[7:15]

    def to_left(x):
        return pltpu.roll(x, width - 1, 1)

    def to_right(x):
        return pltpu.roll(x, 1, 1)

    def prepare(k, carry):
        start = pl.multiple_of(8 * k, 8)
        here = pl.ds(start, 8)
        w = window(eta, start)
        mine = w[8:16]
        nxt, prv = shifts(w)
        y_sum = nxt + prv
        x_sum = to_left(mine) + to_right(mine)
        base = 5.0 * mine + jnp.exp(q[here, :])
        inv_u = OMEGA / (base + 2.0 * x_sum + 0.5 * y_sum)
        inv_v = OMEGA / (base + 2.0 * y_sum + 0.5 * x_sum)
        inv[0, here, :] = inv_u
        inv[1, here, :] = inv_v
        a0[0, here, :] = inv_u * f[0, here, :]
        a0[1, here, :] = inv_v * f[1, here, :]
        return carry

    chunks = (rows + 2 * RH) // 8
    lax.fori_loop(1, 1 + chunks, prepare, 0)

    def sweep(src, start):
        here = pl.ds(start, 8)
        e = window(eta, start)
        u, v = window(src, start, 0), window(src, start, 1)
        gu, gv = e * u, e * v
        em, um, vm = e[8:16], u[8:16], v[8:16]
        gum, gvm = gu[8:16], gv[8:16]
        un, us = shifts(u)
        vn, vs = shifts(v)
        gun, gus = shifts(gu)
        gvn, gvs = shifts(gv)
        du, dv = 0.75 * (un - us), 0.75 * (vn - vs)
        u2, v2 = 2.0 * um, 0.5 * vm
        su = f[0, here, :] + em * (to_left(u2 + dv) + to_right(u2 - dv) + 0.5 * (un + us))
        su = su + 2.0 * (to_left(gum) + to_right(gum)) + 0.5 * (gun + gus)
        sv = f[1, here, :] + em * (to_left(v2 + du) + to_right(v2 - du) + 2.0 * (vn + vs))
        sv = sv + 0.5 * (to_left(gvm) + to_right(gvm)) + 2.0 * (gvn + gvs)
        keep = 1.0 - OMEGA
        return keep * um + inv[0, here, :] * su, keep * vm + inv[1, here, :] * sv

    def second(k, carry):
        start = pl.multiple_of(8 * k, 8)
        u, v = sweep(a0, start)
        a1[0, pl.ds(start, 8), :] = u
        a1[1, pl.ds(start, 8), :] = v
        return carry

    lax.fori_loop(1, 1 + chunks, second, 0)

    @pl.when(ty == 0)
    def _():
        a1[:, R0 - RH : R0, :] = jnp.zeros((2, RH, width), jnp.float32)

    @pl.when(ty == lax.axis_size("ty") - 1)
    def _():
        a1[:, R0 + rows : R0 + rows + RH, :] = jnp.zeros((2, RH, width), jnp.float32)

    @pl.when(tx == 0)
    def _():
        a1[:, :, :CH] = jnp.zeros((2, a1.shape[1], CH), jnp.float32)

    @pl.when(tx == lax.axis_size("tx") - 1)
    def _():
        a1[:, :, CH + cols :] = jnp.zeros((2, a1.shape[1], CH), jnp.float32)

    copies[-1].wait()
    inner = slice(CH, CH + cols)

    def third(k, carry):
        total = jnp.zeros((8, cols), jnp.float32)
        for half in range(CB // 8):
            own = pl.multiple_of(CB * k + 8 * half, 8)
            start = pl.multiple_of(own + R0, 8)
            u, v = sweep(a1, start)
            u, v = u[:, inner], v[:, inner]
            adj_out[0, pl.ds(own, 8), :] = u
            adj_out[1, pl.ds(own, 8), :] = v
            w = window(q, start)
            nxt, prv = shifts(w)
            mine = w[8:16]
            smooth = (4.0 * mine - (to_left(mine) + to_right(mine) + nxt + prv))[:, inner]
            data = vel[0, pl.ds(own, 8), :] * u + vel[1, pl.ds(own, 8), :] * v
            total = total + REGULAR * smooth - jnp.exp(mine[:, inner]) * data
        gsum[pl.ds(pl.multiple_of(8 * k, 8), 8), :] = total
        return carry

    lax.fori_loop(0, rows // CB, third, 0)
    sums = jnp.sum(gsum[...].reshape(rows // CB, 8, cols), axis=1)
    cell = lax.broadcasted_iota(jnp.int32, (cols, cols // CB), 0) // CB
    column = lax.broadcasted_iota(jnp.int32, (cols, cols // CB), 1)
    pick = (cell == column).astype(jnp.float32)
    coarse = jnp.dot(
        sums, pick, preferred_element_type=jnp.float32, precision=lax.Precision.HIGHEST
    )
    share = coarse_out.shape[1]
    for i in range(coarse_out.shape[0]):
        coarse_out[i] = coarse[i * share : (i + 1) * share]


SIDES = [(dy, dx) for dy in (-1, 0, 1) for dx in (-1, 0, 1) if (dy, dx) != (0, 0)]


def present(dy, dx):
    y, x = lax.axis_index("ty") + dy, lax.axis_index("tx") + dx
    inside = (y >= 0) & (y < lax.axis_size("ty")) & (x >= 0) & (x < lax.axis_size("tx"))
    return inside, (y, x)


def edge_spots(dy, dx, core, halo):
    top, bottom, left, right = halo
    rows, cols = core.shape[-2:]
    lead = (slice(None),) * (len(core.shape) - 2)
    y = {-1: pl.ds(0, RH), 0: pl.ds(0, rows), 1: pl.ds(rows - RH, RH)}[dy]
    x = {-1: pl.ds(0, CH), 0: pl.ds(0, cols), 1: pl.ds(cols - CH, CH)}[dx]
    if dx == 0:
        target = top if dy == 1 else bottom
    else:
        strip = left if dx == 1 else right
        span = {1: pl.ds(0, RH), 0: pl.ds(RH, rows), -1: pl.ds(RH + rows, RH)}[dy]
        target = strip.at[lead + (span, slice(None))]
    return core.at[lead + (y, x)], target


def edge_copies(fields, send, recv):
    for i, (dy, dx) in enumerate(SIDES):
        for j, (core, halo) in enumerate(fields):
            src, dst = edge_spots(dy, dx, core, halo)
            there, where = present(dy, dx)
            k = i * len(fields) + j
            copy = pltpu.make_async_remote_copy(
                src_ref=src,
                dst_ref=dst,
                send_sem=send.at[k],
                recv_sem=recv.at[k],
                device_id=where,
                device_id_type=pl.DeviceIdType.MESH,
            )
            yield copy, dst, there, present(-dy, -dx)[0]


def start_edges(fields, send, recv):
    for copy, dst, there, source in edge_copies(fields, send, recv):

        @pl.when(there)
        def _(copy=copy):
            copy.start()

        @pl.when(jnp.logical_not(source))
        def _(dst=dst):
            dst[...] = jnp.zeros(dst.shape, jnp.float32)


def finish_edges(fields, send, recv):
    for copy, _, there, source in edge_copies(fields, send, recv):

        @pl.when(there)
        def _(copy=copy):
            copy.wait_send()

        @pl.when(source)
        def _(copy=copy):
            copy.wait_recv()


def exchange_kernel(
    packed, eta, q, got, et, eb, el, er, qt, qb, ql, qr,
    send, recv, edge_send, edge_recv, local,
):
    devices = packed.shape[0]
    ntx = lax.axis_size("tx")
    me = lax.axis_index("ty") * ntx + lax.axis_index("tx")
    barrier = pltpu.get_barrier_semaphore()

    def place(d):
        target = lax.rem(me + d, devices)
        return target, (target // ntx, lax.rem(target, ntx))

    def greet(d, carry):
        pl.semaphore_signal(
            barrier, inc=1, device_id=place(d)[1], device_id_type=pl.DeviceIdType.MESH
        )
        return carry

    lax.fori_loop(1, devices, greet, 0)
    pl.semaphore_wait(barrier, devices - 1)

    def row_copy(d):
        target, where = place(d)
        return pltpu.make_async_remote_copy(
            src_ref=packed.at[target],
            dst_ref=got.at[me],
            send_sem=send.at[d],
            recv_sem=recv.at[d],
            device_id=where,
            device_id_type=pl.DeviceIdType.MESH,
        )

    def begin(d, carry):
        row_copy(d).start()
        return carry

    lax.fori_loop(1, devices, begin, 0)
    own = pltpu.make_async_copy(packed.at[me], got.at[me], local)
    own.start()
    fields = [(eta, (et, eb, el, er)), (q, (qt, qb, ql, qr))]
    start_edges(fields, edge_send, edge_recv)
    finish_edges(fields, edge_send, edge_recv)
    own.wait()

    def finish(d, carry):
        copy = row_copy(d)
        copy.wait_send()
        copy.wait_recv()
        return carry

    lax.fori_loop(1, devices, finish, 0)


def edge_kernel(f, ft, fb, fl, fr, send, recv):
    barrier = pltpu.get_barrier_semaphore()
    for dy, dx in SIDES:
        there, where = present(dy, dx)

        @pl.when(there)
        def _(where=where):
            pl.semaphore_signal(
                barrier, inc=1, device_id=where, device_id_type=pl.DeviceIdType.MESH
            )

    peers = sum(present(dy, dx)[0].astype(jnp.int32) for dy, dx in SIDES)
    pl.semaphore_wait(barrier, peers)

    fields = [(f, (ft, fb, fl, fr))]
    start_edges(fields, send, recv)
    finish_edges(fields, send, recv)


def coarse_kernel(part, out, held, send, recv):
    count = part.shape[0]
    ty, me = lax.axis_index("ty"), lax.axis_index("tx")
    barrier = pltpu.get_barrier_semaphore()
    for d in range(1, count):
        pl.semaphore_signal(
            barrier,
            inc=1,
            device_id=(ty, lax.rem(me + d, count)),
            device_id_type=pl.DeviceIdType.MESH,
        )
    pl.semaphore_wait(barrier, count - 1)
    copies = []
    for d in range(1, count):
        target = lax.rem(me + d, count)
        copy = pltpu.make_async_remote_copy(
            src_ref=part.at[target],
            dst_ref=held.at[me],
            send_sem=send.at[d],
            recv_sem=recv.at[d],
            device_id=(ty, target),
            device_id_type=pl.DeviceIdType.MESH,
        )
        copy.start()
        copies.append(copy)
    held[me] = part[me]
    for copy in copies:
        copy.wait_send()
        copy.wait_recv()
    width = part.shape[2]
    for i in range(count):
        out[:, i * width : (i + 1) * width] = held[i]


VMEM = pl.BlockSpec(memory_space=pltpu.VMEM)
SMEM = pl.BlockSpec(memory_space=pltpu.SMEM)
ANY = pl.BlockSpec(memory_space=pl.ANY)


def shards(track_rows, track_tile, track_slot, velocity, viscosity, log_friction):
    rows, cols = viscosity.shape
    tiles_x = lax.axis_size("tx")
    devices = lax.axis_size("ty") * tiles_x
    rows_dev, _, seg = track_rows.shape
    cap = max(2, 2 * rows_dev // devices)
    params = pltpu.CompilerParams(vmem_limit_bytes=VMEM_LIMIT)
    f32 = jnp.float32
    block = track_rows.reshape(rows_dev, 2, 2, 128).transpose(0, 2, 1, 3).reshape(rows_dev, 4, 128)
    packed = pl.pallas_call(
        functools.partial(pack_kernel, cap),
        out_shape=jax.ShapeDtypeStruct((devices, cap + 1, 4, 128), f32),
        in_specs=[SMEM, SMEM, VMEM],
        out_specs=VMEM,
        scratch_shapes=[pltpu.SMEM((devices,), jnp.int32)],
        compiler_params=params,
        name="pack",
    )(track_tile[:, 0], track_slot, block)
    halo = [(RH, cols), (RH, cols), (rows + 2 * RH, CH), (rows + 2 * RH, CH)]

    def remote(number):
        return pltpu.CompilerParams(
            collective_id=number, has_side_effects=True, vmem_limit_bytes=VMEM_LIMIT
        )

    got, *eq_halo = pl.pallas_call(
        exchange_kernel,
        out_shape=[jax.ShapeDtypeStruct(packed.shape, f32)]
        + [jax.ShapeDtypeStruct(shape, f32) for shape in halo * 2],
        in_specs=[ANY] * 3,
        out_specs=[ANY] + [VMEM] * 8,
        scratch_shapes=[
            pltpu.SemaphoreType.DMA((devices,)),
            pltpu.SemaphoreType.DMA((devices,)),
            pltpu.SemaphoreType.DMA((16,)),
            pltpu.SemaphoreType.DMA((16,)),
            pltpu.SemaphoreType.DMA,
        ],
        compiler_params=remote(0),
        name="exchange",
    )(packed, viscosity, log_friction)
    meta = got[:, cap, 0, :].astype(jnp.int32).reshape(devices * 128)
    forcing = pl.pallas_call(
        functools.partial(scatter_kernel, cap, cols // seg),
        out_shape=jax.ShapeDtypeStruct((2, rows, cols), f32),
        in_specs=[SMEM, VMEM],
        out_specs=VMEM,
        compiler_params=params,
        name="scatter",
    )(meta, got)
    f_halo = pl.pallas_call(
        edge_kernel,
        out_shape=[jax.ShapeDtypeStruct((2,) + shape, f32) for shape in halo],
        in_specs=[ANY],
        out_specs=[VMEM] * 4,
        scratch_shapes=[pltpu.SemaphoreType.DMA((8,)), pltpu.SemaphoreType.DMA((8,))],
        compiler_params=remote(1),
        name="edges",
    )(forcing)
    coarse_rows = rows // CB
    big = (rows + 2 * R0, cols + 2 * CH)
    adjoint, coarse = pl.pallas_call(
        stencil_kernel,
        out_shape=(
            jax.ShapeDtypeStruct((2, rows, cols), f32),
            jax.ShapeDtypeStruct((tiles_x, coarse_rows // tiles_x, cols // CB), f32),
        ),
        in_specs=[ANY] * 16,
        out_specs=(VMEM, VMEM),
        scratch_shapes=[
            pltpu.VMEM((2,) + big, f32),
            pltpu.VMEM(big, f32),
            pltpu.VMEM(big, f32),
            pltpu.VMEM((2,) + big, f32),
            pltpu.VMEM((2,) + big, f32),
            pltpu.VMEM((2,) + big, f32),
            pltpu.VMEM((2, rows, cols), f32),
            pltpu.VMEM((coarse_rows * 8, cols), f32),
            pltpu.SemaphoreType.DMA((21,)),
        ],
        compiler_params=params,
        name="stencil",
    )(forcing, *f_halo, viscosity, log_friction, *eq_halo, velocity)
    grad = pl.pallas_call(
        coarse_kernel,
        out_shape=jax.ShapeDtypeStruct((coarse_rows // tiles_x, cols // CB * tiles_x), f32),
        in_specs=[VMEM],
        out_specs=VMEM,
        scratch_shapes=[
            pltpu.VMEM(coarse.shape, f32),
            pltpu.SemaphoreType.DMA((tiles_x,)),
            pltpu.SemaphoreType.DMA((tiles_x,)),
        ],
        compiler_params=remote(2),
        name="coarse",
    )(coarse)
    return adjoint, grad


def solution(mesh):
    return jax.shard_map(
        shards,
        mesh=mesh,
        in_specs=(
            P(("ty", "tx"), None, None),
            P(("ty", "tx"), None),
            P(("ty", "tx")),
            P(None, "ty", "tx"),
            P("ty", "tx"),
            P("ty", "tx"),
        ),
        out_specs=(P(None, "ty", "tx"), P(("ty", "tx"), None)),
        check_vma=False,
    )
```

```python
import functools

import jax
import jax.numpy as jnp
from jax import lax
from jax.experimental import pallas as pl
from jax.experimental.pallas import tpu as pltpu
from jax.sharding import PartitionSpec as P

CB = 16
OMEGA = 0.8
REGULAR = 0.1
RH = 8
CH = 128
R0 = 16
VMEM_LIMIT = 56 * 1024 * 1024


def compact(fields):
    half = RH // 2
    north = [top[:half] for top, _, _, _ in fields]
    south = [bottom[half:] for _, bottom, _, _ in fields]
    west = [left.T[:half] for _, _, left, _ in fields]
    east = [right.T[CH - half :] for _, _, _, right in fields]
    return [jnp.concatenate(parts, axis=0) for parts in (north, south, west, east)]


def pack_kernel(
    cap, tile_ref, slot_ref, rows_ref, eta_in, q_in,
    out_ref, north, south, west, east,
    count, row_edges, col_edges, sems,
):
    devices = out_ref.shape[0]
    rows, cols = eta_in.shape
    copies = []
    for i, x in enumerate((eta_in, q_in)):
        spots = (
            (x.at[pl.ds(0, RH), :], row_edges.at[2 * i]),
            (x.at[pl.ds(rows - RH, RH), :], row_edges.at[2 * i + 1]),
            (x.at[:, pl.ds(0, CH)], col_edges.at[2 * i]),
            (x.at[:, pl.ds(cols - CH, CH)], col_edges.at[2 * i + 1]),
        )
        for j, (src, dst) in enumerate(spots):
            copies.append(pltpu.make_async_copy(src, dst, sems.at[4 * i + j]))
    for copy in copies:
        copy.start()
    lanes = lax.broadcasted_iota(jnp.int32, (4, 128), 1)

    def clear(d, carry):
        count[d] = 0
        out_ref[d, cap] = jnp.zeros((4, 128), jnp.float32)
        return carry

    lax.fori_loop(0, devices, clear, 0)

    def place(i, carry):
        t = tile_ref[i]
        r = count[t]
        count[t] = r + 1
        out_ref[t, r] = rows_ref[i]
        slot = slot_ref[i].astype(jnp.float32)
        filled = (r + 1).astype(jnp.float32)
        head = out_ref[t, cap]
        out_ref[t, cap] = jnp.where(lanes == r, slot, jnp.where(lanes == cap, filled, head))
        return carry

    lax.fori_loop(0, rows_ref.shape[0], place, 0)
    for copy in copies:
        copy.wait()
    fields = [
        (row_edges[2 * i], row_edges[2 * i + 1], col_edges[2 * i], col_edges[2 * i + 1])
        for i in range(2)
    ]
    for ref, value in zip((north, south, west, east), compact(fields)):
        ref[...] = value


def scatter_kernel(cap, segs, meta_ref, got_ref, out_ref, north, south, west, east):
    out_ref[...] = jnp.zeros_like(out_ref)
    lanes = lax.broadcasted_iota(jnp.int32, (8, 128), 0)

    def source(s, carry):
        def add(r, inner):
            slot = meta_ref[s * 128 + r]
            y = slot // segs
            x = pl.multiple_of((slot % segs) * 256, 256)
            base = pl.multiple_of(y // 8 * 8, 8)
            chosen = lanes == y % 8
            spots = [(c, pl.ds(base, 8), pl.ds(x + 128 * h, 128)) for h in range(2) for c in range(2)]
            olds = [out_ref[spot] for spot in spots]
            news = [got_ref[s, r, pl.ds(j, 1), :] for j in range(4)]
            for spot, old, new in zip(spots, olds, news):
                out_ref[spot] = old + jnp.where(chosen, new, 0.0)
            return inner

        return lax.fori_loop(0, meta_ref[s * 128 + cap], add, carry)

    lax.fori_loop(0, got_ref.shape[0], source, 0)
    _, rows, cols = out_ref.shape
    fields = [
        (
            out_ref[c, :RH, :],
            out_ref[c, rows - RH :, :],
            out_ref[c, :, :CH],
            out_ref[c, :, cols - CH :],
        )
        for c in range(2)
    ]
    for ref, value in zip((north, south, west, east), compact(fields)):
        ref[...] = value


def stencil_kernel(
    f_in, ft, fb, fl, fr, fc, eta_in, q_in, et, eb, el, er, ec, vel_in,
    adj_out, coarse_out,
    f, eta, q, a0, a1, inv, vel, gsum, sems,
):
    _, rows, cols = f_in.shape
    width = cols + 2 * CH
    ty, tx = lax.axis_index("ty"), lax.axis_index("tx")
    mid = (pl.ds(R0, rows), pl.ds(CH, cols))
    moves = [(eta_in, eta.at[mid]), (q_in, q.at[mid])]
    for c in range(2):
        moves.append((f_in.at[c], f.at[(c,) + mid]))
    n_second = len(moves)
    moves.append((vel_in, vel))
    copies = [pltpu.make_async_copy(a, b, sems.at[i]) for i, (a, b) in enumerate(moves)]
    for copy in copies:
        copy.start()
    half = RH // 2
    above, below = slice(R0 - RH, R0), slice(R0 + rows, R0 + rows + RH)
    core, first, last = slice(CH, CH + cols), slice(0, CH), slice(CH + cols, width)

    def spread(i, edges, put):
        top, bottom, left, right, corner = edges
        own = slice(half * i, half * i + half)
        for span, x, block in (
            (above, core, top[own, :]),
            (below, core, bottom[own, :]),
            (above, first, corner[0, own, :]),
            (above, last, corner[1, own, :]),
            (below, first, corner[2, own, :]),
            (below, last, corner[3, own, :]),
        ):
            rest = jnp.zeros_like(block)
            parts = [rest, block] if span == above else [block, rest]
            put(span, x, jnp.concatenate(parts, axis=0))
        rest = jnp.zeros((CH - half, rows), jnp.float32)
        tall = slice(R0, R0 + rows)
        put(tall, first, jnp.concatenate([rest, left[own, :]], axis=0).T)
        put(tall, last, jnp.concatenate([right[own, :], rest], axis=0).T)

    def put_into(ref, *lead):
        def put(y, x, value):
            ref[lead + (y, x)] = value

        return put

    for i in range(2):
        spread(i, (et, eb, el, er, ec), put_into((eta, q)[i]))
        spread(i, (ft, fb, fl, fr, fc), put_into(f, i))
    for copy in copies[:n_second]:
        copy.wait()

    def window(ref, start, *lead):
        return ref[lead + (pl.ds(start - 8, 24), slice(None))]

    def shifts(w):
        return w[9:17], w[7:15]

    def to_left(x):
        return pltpu.roll(x, width - 1, 1)

    def to_right(x):
        return pltpu.roll(x, 1, 1)

    def prepare(k, carry):
        start = pl.multiple_of(8 * k, 8)
        here = pl.ds(start, 8)
        w = window(eta, start)
        mine = w[8:16]
        nxt, prv = shifts(w)
        y_sum = nxt + prv
        x_sum = to_left(mine) + to_right(mine)
        base = 5.0 * mine + jnp.exp(q[here, :])
        inv_u = OMEGA / (base + 2.0 * x_sum + 0.5 * y_sum)
        inv_v = OMEGA / (base + 2.0 * y_sum + 0.5 * x_sum)
        inv[0, here, :] = inv_u
        inv[1, here, :] = inv_v
        a0[0, here, :] = inv_u * f[0, here, :]
        a0[1, here, :] = inv_v * f[1, here, :]
        return carry

    chunks = (rows + 2 * RH) // 8
    lax.fori_loop(1, 1 + chunks, prepare, 0)

    def sweep(src, start):
        here = pl.ds(start, 8)
        e = window(eta, start)
        u, v = window(src, start, 0), window(src, start, 1)
        gu, gv = e * u, e * v
        em, um, vm = e[8:16], u[8:16], v[8:16]
        gum, gvm = gu[8:16], gv[8:16]
        un, us = shifts(u)
        vn, vs = shifts(v)
        gun, gus = shifts(gu)
        gvn, gvs = shifts(gv)
        du, dv = 0.75 * (un - us), 0.75 * (vn - vs)
        u2, v2 = 2.0 * um, 0.5 * vm
        su = f[0, here, :] + em * (to_left(u2 + dv) + to_right(u2 - dv) + 0.5 * (un + us))
        su = su + 2.0 * (to_left(gum) + to_right(gum)) + 0.5 * (gun + gus)
        sv = f[1, here, :] + em * (to_left(v2 + du) + to_right(v2 - du) + 2.0 * (vn + vs))
        sv = sv + 0.5 * (to_left(gvm) + to_right(gvm)) + 2.0 * (gvn + gvs)
        keep = 1.0 - OMEGA
        return keep * um + inv[0, here, :] * su, keep * vm + inv[1, here, :] * sv

    def second(k, carry):
        start = pl.multiple_of(8 * k, 8)
        u, v = sweep(a0, start)
        a1[0, pl.ds(start, 8), :] = u
        a1[1, pl.ds(start, 8), :] = v
        return carry

    lax.fori_loop(1, 1 + chunks, second, 0)

    @pl.when(ty == 0)
    def _():
        a1[:, R0 - RH : R0, :] = jnp.zeros((2, RH, width), jnp.float32)

    @pl.when(ty == lax.axis_size("ty") - 1)
    def _():
        a1[:, R0 + rows : R0 + rows + RH, :] = jnp.zeros((2, RH, width), jnp.float32)

    @pl.when(tx == 0)
    def _():
        a1[:, :, :CH] = jnp.zeros((2, a1.shape[1], CH), jnp.float32)

    @pl.when(tx == lax.axis_size("tx") - 1)
    def _():
        a1[:, :, CH + cols :] = jnp.zeros((2, a1.shape[1], CH), jnp.float32)

    copies[-1].wait()
    inner = slice(CH, CH + cols)

    def third(k, carry):
        total = jnp.zeros((8, cols), jnp.float32)
        for half in range(CB // 8):
            own = pl.multiple_of(CB * k + 8 * half, 8)
            start = pl.multiple_of(own + R0, 8)
            u, v = sweep(a1, start)
            u, v = u[:, inner], v[:, inner]
            adj_out[0, pl.ds(own, 8), :] = u
            adj_out[1, pl.ds(own, 8), :] = v
            w = window(q, start)
            nxt, prv = shifts(w)
            mine = w[8:16]
            smooth = (4.0 * mine - (to_left(mine) + to_right(mine) + nxt + prv))[:, inner]
            data = vel[0, pl.ds(own, 8), :] * u + vel[1, pl.ds(own, 8), :] * v
            total = total + REGULAR * smooth - jnp.exp(mine[:, inner]) * data
        gsum[pl.ds(pl.multiple_of(8 * k, 8), 8), :] = total
        return carry

    lax.fori_loop(0, rows // CB, third, 0)
    sums = jnp.sum(gsum[...].reshape(rows // CB, 8, cols), axis=1)
    cell = lax.broadcasted_iota(jnp.int32, (cols, cols // CB), 0) // CB
    column = lax.broadcasted_iota(jnp.int32, (cols, cols // CB), 1)
    pick = (cell == column).astype(jnp.float32)
    coarse = jnp.dot(
        sums, pick, preferred_element_type=jnp.float32, precision=lax.Precision.HIGHEST
    )
    share = coarse_out.shape[1]
    for i in range(coarse_out.shape[0]):
        coarse_out[i] = coarse[i * share : (i + 1) * share]


SIDES = [(dy, dx) for dy in (-1, 0, 1) for dx in (-1, 0, 1) if (dy, dx) != (0, 0)]


def present(dy, dx):
    y, x = lax.axis_index("ty") + dy, lax.axis_index("tx") + dx
    inside = (y >= 0) & (y < lax.axis_size("ty")) & (x >= 0) & (x < lax.axis_size("tx"))
    return inside, (y, x)


def edge_spots(dy, dx, core, halo):
    north, south, west, east = core
    top, bottom, left, right, corner = halo
    if dx == 0:
        return (north, bottom) if dy == -1 else (south, top)
    if dy == 0:
        return (west, right) if dx == -1 else (east, left)
    src = north if dy == -1 else south
    start = 0 if dx == -1 else src.shape[1] - CH
    k = (0 if dy == 1 else 2) + (0 if dx == 1 else 1)
    return src.at[:, pl.ds(start, CH)], corner.at[k]


def edge_copies(core, halo, send, recv):
    for k, (dy, dx) in enumerate(SIDES):
        src, dst = edge_spots(dy, dx, core, halo)
        there, where = present(dy, dx)
        copy = pltpu.make_async_remote_copy(
            src_ref=src,
            dst_ref=dst,
            send_sem=send.at[k],
            recv_sem=recv.at[k],
            device_id=where,
            device_id_type=pl.DeviceIdType.MESH,
        )
        yield copy, dst, there, present(-dy, -dx)[0]


def start_edges(core, halo, send, recv):
    for copy, dst, there, source in edge_copies(core, halo, send, recv):

        @pl.when(there)
        def _(copy=copy):
            copy.start()

        @pl.when(jnp.logical_not(source))
        def _(dst=dst):
            dst[...] = jnp.zeros(dst.shape, jnp.float32)


def finish_edges(core, halo, send, recv):
    for copy, _, there, source in edge_copies(core, halo, send, recv):

        @pl.when(there)
        def _(copy=copy):
            copy.wait_send()

        @pl.when(source)
        def _(copy=copy):
            copy.wait_recv()


def exchange_kernel(
    packed, north, south, west, east, got, top, bottom, left, right, corner,
    send, recv, edge_send, edge_recv, local,
):
    devices = packed.shape[0]
    ntx = lax.axis_size("tx")
    me = lax.axis_index("ty") * ntx + lax.axis_index("tx")
    barrier = pltpu.get_barrier_semaphore()

    def place(d):
        target = lax.rem(me + d, devices)
        return target, (target // ntx, lax.rem(target, ntx))

    def greet(d, carry):
        pl.semaphore_signal(
            barrier, inc=1, device_id=place(d)[1], device_id_type=pl.DeviceIdType.MESH
        )
        return carry

    lax.fori_loop(1, devices, greet, 0)
    pl.semaphore_wait(barrier, devices - 1)

    def row_copy(d):
        target, where = place(d)
        return pltpu.make_async_remote_copy(
            src_ref=packed.at[target],
            dst_ref=got.at[me],
            send_sem=send.at[d],
            recv_sem=recv.at[d],
            device_id=where,
            device_id_type=pl.DeviceIdType.MESH,
        )

    def begin(d, carry):
        row_copy(d).start()
        return carry

    lax.fori_loop(1, devices, begin, 0)
    own = pltpu.make_async_copy(packed.at[me], got.at[me], local)
    own.start()
    edges = ((north, south, west, east), (top, bottom, left, right, corner))
    start_edges(*edges, edge_send, edge_recv)
    finish_edges(*edges, edge_send, edge_recv)
    own.wait()

    def finish(d, carry):
        copy = row_copy(d)
        copy.wait_send()
        copy.wait_recv()
        return carry

    lax.fori_loop(1, devices, finish, 0)


def edge_kernel(north, south, west, east, top, bottom, left, right, corner, send, recv):
    barrier = pltpu.get_barrier_semaphore()
    for dy, dx in SIDES:
        there, where = present(dy, dx)

        @pl.when(there)
        def _(where=where):
            pl.semaphore_signal(
                barrier, inc=1, device_id=where, device_id_type=pl.DeviceIdType.MESH
            )

    peers = sum(present(dy, dx)[0].astype(jnp.int32) for dy, dx in SIDES)
    pl.semaphore_wait(barrier, peers)

    edges = ((north, south, west, east), (top, bottom, left, right, corner))
    start_edges(*edges, send, recv)
    finish_edges(*edges, send, recv)


def coarse_kernel(part, out, held, send, recv):
    count = part.shape[0]
    ty, me = lax.axis_index("ty"), lax.axis_index("tx")
    barrier = pltpu.get_barrier_semaphore()
    for d in range(1, count):
        pl.semaphore_signal(
            barrier,
            inc=1,
            device_id=(ty, lax.rem(me + d, count)),
            device_id_type=pl.DeviceIdType.MESH,
        )
    pl.semaphore_wait(barrier, count - 1)
    copies = []
    for d in range(1, count):
        target = lax.rem(me + d, count)
        copy = pltpu.make_async_remote_copy(
            src_ref=part.at[target],
            dst_ref=held.at[me],
            send_sem=send.at[d],
            recv_sem=recv.at[d],
            device_id=(ty, target),
            device_id_type=pl.DeviceIdType.MESH,
        )
        copy.start()
        copies.append(copy)
    held[me] = part[me]
    for copy in copies:
        copy.wait_send()
        copy.wait_recv()
    width = part.shape[2]
    for i in range(count):
        out[:, i * width : (i + 1) * width] = held[i]


VMEM = pl.BlockSpec(memory_space=pltpu.VMEM)
SMEM = pl.BlockSpec(memory_space=pltpu.SMEM)
ANY = pl.BlockSpec(memory_space=pl.ANY)


def shards(track_rows, track_tile, track_slot, velocity, viscosity, log_friction):
    rows, cols = viscosity.shape
    tiles_x = lax.axis_size("tx")
    devices = lax.axis_size("ty") * tiles_x
    rows_dev, _, seg = track_rows.shape
    cap = max(2, 2 * rows_dev // devices)
    params = pltpu.CompilerParams(vmem_limit_bytes=VMEM_LIMIT)
    f32 = jnp.float32
    block = track_rows.reshape(rows_dev, 2, 2, 128).transpose(0, 2, 1, 3).reshape(rows_dev, 4, 128)
    edge_shapes = [
        jax.ShapeDtypeStruct(shape, f32) for shape in ((RH, cols),) * 2 + ((RH, rows),) * 2
    ]
    halo_shapes = edge_shapes + [jax.ShapeDtypeStruct((4, RH, CH), f32)]
    packed, *eq_edges = pl.pallas_call(
        functools.partial(pack_kernel, cap),
        out_shape=[jax.ShapeDtypeStruct((devices, cap + 1, 4, 128), f32)] + edge_shapes,
        in_specs=[SMEM, SMEM, VMEM, ANY, ANY],
        out_specs=[VMEM] * 5,
        scratch_shapes=[
            pltpu.SMEM((devices,), jnp.int32),
            pltpu.VMEM((4, RH, cols), f32),
            pltpu.VMEM((4, rows, CH), f32),
            pltpu.SemaphoreType.DMA((8,)),
        ],
        compiler_params=params,
        name="pack",
    )(track_tile[:, 0], track_slot, block, viscosity, log_friction)

    def remote(number):
        return pltpu.CompilerParams(
            collective_id=number, has_side_effects=True, vmem_limit_bytes=VMEM_LIMIT
        )

    got, *eq_halo = pl.pallas_call(
        exchange_kernel,
        out_shape=[jax.ShapeDtypeStruct(packed.shape, f32)] + halo_shapes,
        in_specs=[ANY] + [VMEM] * 4,
        out_specs=[ANY] + [VMEM] * 5,
        scratch_shapes=[
            pltpu.SemaphoreType.DMA((devices,)),
            pltpu.SemaphoreType.DMA((devices,)),
            pltpu.SemaphoreType.DMA((8,)),
            pltpu.SemaphoreType.DMA((8,)),
            pltpu.SemaphoreType.DMA,
        ],
        compiler_params=remote(0),
        name="exchange",
    )(packed, *eq_edges)
    meta = got[:, cap, 0, :].astype(jnp.int32).reshape(devices * 128)
    forcing, *f_edges = pl.pallas_call(
        functools.partial(scatter_kernel, cap, cols // seg),
        out_shape=[jax.ShapeDtypeStruct((2, rows, cols), f32)] + edge_shapes,
        in_specs=[SMEM, VMEM],
        out_specs=[VMEM] * 5,
        compiler_params=params,
        name="scatter",
    )(meta, got)
    f_halo = pl.pallas_call(
        edge_kernel,
        out_shape=halo_shapes,
        in_specs=[VMEM] * 4,
        out_specs=[VMEM] * 5,
        scratch_shapes=[pltpu.SemaphoreType.DMA((8,)), pltpu.SemaphoreType.DMA((8,))],
        compiler_params=remote(1),
        name="edges",
    )(*f_edges)
    coarse_rows = rows // CB
    big = (rows + 2 * R0, cols + 2 * CH)
    adjoint, coarse = pl.pallas_call(
        stencil_kernel,
        out_shape=(
            jax.ShapeDtypeStruct((2, rows, cols), f32),
            jax.ShapeDtypeStruct((tiles_x, coarse_rows // tiles_x, cols // CB), f32),
        ),
        in_specs=[ANY] + [VMEM] * 5 + [ANY] * 2 + [VMEM] * 5 + [ANY],
        out_specs=(VMEM, VMEM),
        scratch_shapes=[
            pltpu.VMEM((2,) + big, f32),
            pltpu.VMEM(big, f32),
            pltpu.VMEM(big, f32),
            pltpu.VMEM((2,) + big, f32),
            pltpu.VMEM((2,) + big, f32),
            pltpu.VMEM((2,) + big, f32),
            pltpu.VMEM((2, rows, cols), f32),
            pltpu.VMEM((coarse_rows * 8, cols), f32),
            pltpu.SemaphoreType.DMA((5,)),
        ],
        compiler_params=params,
        name="stencil",
    )(forcing, *f_halo, viscosity, log_friction, *eq_halo, velocity)
    grad = pl.pallas_call(
        coarse_kernel,
        out_shape=jax.ShapeDtypeStruct((coarse_rows // tiles_x, cols // CB * tiles_x), f32),
        in_specs=[VMEM],
        out_specs=VMEM,
        scratch_shapes=[
            pltpu.VMEM(coarse.shape, f32),
            pltpu.SemaphoreType.DMA((tiles_x,)),
            pltpu.SemaphoreType.DMA((tiles_x,)),
        ],
        compiler_params=remote(2),
        name="coarse",
    )(coarse)
    return adjoint, grad


def solution(mesh):
    return jax.shard_map(
        shards,
        mesh=mesh,
        in_specs=(
            P(("ty", "tx"), None, None),
            P(("ty", "tx"), None),
            P(("ty", "tx")),
            P(None, "ty", "tx"),
            P("ty", "tx"),
            P("ty", "tx"),
        ),
        out_specs=(P(None, "ty", "tx"), P(("ty", "tx"), None)),
        check_vma=False,
    )
```

```python
import functools

import jax
import jax.numpy as jnp
from jax import lax
from jax.experimental import pallas as pl
from jax.experimental.pallas import tpu as pltpu
from jax.sharding import PartitionSpec as P

CB = 16
OMEGA = 0.8
REGULAR = 0.1
RH = 8
CH = 128
R0 = 16
VMEM_LIMIT = 56 * 1024 * 1024


def compact(fields):
    half = RH // 2
    north = [top[:half] for top, _, _, _ in fields]
    south = [bottom[half:] for _, bottom, _, _ in fields]
    west = [left.T[:half] for _, _, left, _ in fields]
    east = [right.T[CH - half :] for _, _, _, right in fields]
    return [jnp.concatenate(parts, axis=0) for parts in (north, south, west, east)]


def pack_kernel(
    cap, tile_ref, slot_ref, rows_ref, eta_in, q_in,
    out_ref, north, south, west, east,
    count, row_edges, col_edges, sems,
):
    devices = out_ref.shape[0]
    rows, cols = eta_in.shape
    copies = []
    for i, x in enumerate((eta_in, q_in)):
        spots = (
            (x.at[pl.ds(0, RH), :], row_edges.at[2 * i]),
            (x.at[pl.ds(rows - RH, RH), :], row_edges.at[2 * i + 1]),
            (x.at[:, pl.ds(0, CH)], col_edges.at[2 * i]),
            (x.at[:, pl.ds(cols - CH, CH)], col_edges.at[2 * i + 1]),
        )
        for j, (src, dst) in enumerate(spots):
            copies.append(pltpu.make_async_copy(src, dst, sems.at[4 * i + j]))
    for copy in copies:
        copy.start()
    lanes = lax.broadcasted_iota(jnp.int32, (4, 128), 1)

    def clear(d, carry):
        count[d] = 0
        out_ref[d, cap] = jnp.zeros((4, 128), jnp.float32)
        return carry

    lax.fori_loop(0, devices, clear, 0)

    def place(i, carry):
        t = tile_ref[i]
        r = count[t]
        count[t] = r + 1
        out_ref[t, r] = rows_ref[i]
        slot = slot_ref[i].astype(jnp.float32)
        filled = (r + 1).astype(jnp.float32)
        head = out_ref[t, cap]
        out_ref[t, cap] = jnp.where(lanes == r, slot, jnp.where(lanes == cap, filled, head))
        return carry

    lax.fori_loop(0, rows_ref.shape[0], place, 0, unroll=4)
    for copy in copies:
        copy.wait()
    fields = [
        (row_edges[2 * i], row_edges[2 * i + 1], col_edges[2 * i], col_edges[2 * i + 1])
        for i in range(2)
    ]
    for ref, value in zip((north, south, west, east), compact(fields)):
        ref[...] = value


def scatter_kernel(cap, segs, meta_ref, got_ref, out_ref, north, south, west, east, second):
    out_ref[...] = jnp.zeros_like(out_ref)
    lanes = lax.broadcasted_iota(jnp.int32, (8, 128), 0)

    second[...] = jnp.zeros_like(second)
    step = 4 if cap % 4 == 0 else 2 if cap % 2 == 0 else 1

    def source(s, carry):
        filled = meta_ref[s * 128 + cap]

        def add(k, inner):
            spots, news = [], []
            for i in range(step):
                r = k * step + i
                slot = meta_ref[s * 128 + r]
                y = slot // segs
                x = pl.multiple_of((slot - y * segs) * 256, 256)
                base = pl.multiple_of(y // 8 * 8, 8)
                chosen = lanes == jnp.where(r < filled, y - base, -1)
                spots.append(
                    [(c, pl.ds(base, 8), pl.ds(x + 128 * h, 128)) for h in range(2) for c in range(2)]
                )
                row = [got_ref[s, r, pl.ds(j, 1), :] for j in range(4)]
                news.append([jnp.where(chosen, part, 0.0) for part in row])
            for i in range(0, step, 2):
                pairs = list(zip((out_ref, second), spots[i : i + 2], news[i : i + 2]))
                sums = [
                    [ref[spot] + new for spot, new in zip(where, what)] for ref, where, what in pairs
                ]
                for (ref, where, _), values in zip(pairs, sums):
                    for spot, value in zip(where, values):
                        ref[spot] = value
            return inner

        return lax.fori_loop(0, (filled + step - 1) // step, add, carry)

    lax.fori_loop(0, got_ref.shape[0], source, 0)
    out_ref[...] += second[...]
    _, rows, cols = out_ref.shape
    fields = [
        (
            out_ref[c, :RH, :],
            out_ref[c, rows - RH :, :],
            out_ref[c, :, :CH],
            out_ref[c, :, cols - CH :],
        )
        for c in range(2)
    ]
    for ref, value in zip((north, south, west, east), compact(fields)):
        ref[...] = value


def stencil_kernel(
    f_in, ft, fb, fl, fr, fc, eta_in, q_in, et, eb, el, er, ec, vel_in,
    adj_out, coarse_out,
    f, eta, q, a0, a1, inv, vel, gsum, sems,
):
    _, rows, cols = f_in.shape
    width = cols + 2 * CH
    ty, tx = lax.axis_index("ty"), lax.axis_index("tx")
    mid = (pl.ds(R0, rows), pl.ds(CH, cols))
    moves = [(eta_in, eta.at[mid]), (q_in, q.at[mid])]
    for c in range(2):
        moves.append((f_in.at[c], f.at[(c,) + mid]))
    n_second = len(moves)
    moves.append((vel_in, vel))
    copies = [pltpu.make_async_copy(a, b, sems.at[i]) for i, (a, b) in enumerate(moves)]
    for copy in copies:
        copy.start()
    half = RH // 2
    above, below = slice(R0 - RH, R0), slice(R0 + rows, R0 + rows + RH)
    core, first, last = slice(CH, CH + cols), slice(0, CH), slice(CH + cols, width)

    def spread(i, edges, put):
        top, bottom, left, right, corner = edges
        own = slice(half * i, half * i + half)
        for span, x, block in (
            (above, core, top[own, :]),
            (below, core, bottom[own, :]),
            (above, first, corner[0, own, :]),
            (above, last, corner[1, own, :]),
            (below, first, corner[2, own, :]),
            (below, last, corner[3, own, :]),
        ):
            rest = jnp.zeros_like(block)
            parts = [rest, block] if span == above else [block, rest]
            put(span, x, jnp.concatenate(parts, axis=0))
        rest = jnp.zeros((CH - half, rows), jnp.float32)
        tall = slice(R0, R0 + rows)
        put(tall, first, jnp.concatenate([rest, left[own, :]], axis=0).T)
        put(tall, last, jnp.concatenate([right[own, :], rest], axis=0).T)

    def put_into(ref, *lead):
        def put(y, x, value):
            ref[lead + (y, x)] = value

        return put

    for i in range(2):
        spread(i, (et, eb, el, er, ec), put_into((eta, q)[i]))
        spread(i, (ft, fb, fl, fr, fc), put_into(f, i))
    for copy in copies[:n_second]:
        copy.wait()

    def window(ref, start, *lead):
        return ref[lead + (pl.ds(start - 8, 24), slice(None))]

    def shifts(w):
        return w[9:17], w[7:15]

    def to_left(x):
        return pltpu.roll(x, width - 1, 1)

    def to_right(x):
        return pltpu.roll(x, 1, 1)

    def prepare(k, carry):
        start = pl.multiple_of(8 * k, 8)
        here = pl.ds(start, 8)
        w = window(eta, start)
        mine = w[8:16]
        nxt, prv = shifts(w)
        y_sum = nxt + prv
        x_sum = to_left(mine) + to_right(mine)
        base = 5.0 * mine + jnp.exp(q[here, :])
        inv_u = OMEGA / (base + 2.0 * x_sum + 0.5 * y_sum)
        inv_v = OMEGA / (base + 2.0 * y_sum + 0.5 * x_sum)
        inv[0, here, :] = inv_u
        inv[1, here, :] = inv_v
        a0[0, here, :] = inv_u * f[0, here, :]
        a0[1, here, :] = inv_v * f[1, here, :]
        return carry

    chunks = (rows + 2 * RH) // 8
    lax.fori_loop(1, 1 + chunks, prepare, 0)

    def sweep(src, start):
        here = pl.ds(start, 8)
        e = window(eta, start)
        u, v = window(src, start, 0), window(src, start, 1)
        gu, gv = e * u, e * v
        em, um, vm = e[8:16], u[8:16], v[8:16]
        gum, gvm = gu[8:16], gv[8:16]
        un, us = shifts(u)
        vn, vs = shifts(v)
        gun, gus = shifts(gu)
        gvn, gvs = shifts(gv)
        du, dv = 0.75 * (un - us), 0.75 * (vn - vs)
        u2, v2 = 2.0 * um, 0.5 * vm
        su = f[0, here, :] + em * (to_left(u2 + dv) + to_right(u2 - dv) + 0.5 * (un + us))
        su = su + 2.0 * (to_left(gum) + to_right(gum)) + 0.5 * (gun + gus)
        sv = f[1, here, :] + em * (to_left(v2 + du) + to_right(v2 - du) + 2.0 * (vn + vs))
        sv = sv + 0.5 * (to_left(gvm) + to_right(gvm)) + 2.0 * (gvn + gvs)
        keep = 1.0 - OMEGA
        return keep * um + inv[0, here, :] * su, keep * vm + inv[1, here, :] * sv

    def second(k, carry):
        start = pl.multiple_of(8 * k, 8)
        u, v = sweep(a0, start)
        a1[0, pl.ds(start, 8), :] = u
        a1[1, pl.ds(start, 8), :] = v
        return carry

    lax.fori_loop(1, 1 + chunks, second, 0)

    @pl.when(ty == 0)
    def _():
        a1[:, R0 - RH : R0, :] = jnp.zeros((2, RH, width), jnp.float32)

    @pl.when(ty == lax.axis_size("ty") - 1)
    def _():
        a1[:, R0 + rows : R0 + rows + RH, :] = jnp.zeros((2, RH, width), jnp.float32)

    @pl.when(tx == 0)
    def _():
        a1[:, :, :CH] = jnp.zeros((2, a1.shape[1], CH), jnp.float32)

    @pl.when(tx == lax.axis_size("tx") - 1)
    def _():
        a1[:, :, CH + cols :] = jnp.zeros((2, a1.shape[1], CH), jnp.float32)

    copies[-1].wait()
    inner = slice(CH, CH + cols)

    def third(k, carry):
        total = jnp.zeros((8, cols), jnp.float32)
        for half in range(CB // 8):
            own = pl.multiple_of(CB * k + 8 * half, 8)
            start = pl.multiple_of(own + R0, 8)
            u, v = sweep(a1, start)
            u, v = u[:, inner], v[:, inner]
            adj_out[0, pl.ds(own, 8), :] = u
            adj_out[1, pl.ds(own, 8), :] = v
            w = window(q, start)
            nxt, prv = shifts(w)
            mine = w[8:16]
            smooth = (4.0 * mine - (to_left(mine) + to_right(mine) + nxt + prv))[:, inner]
            data = vel[0, pl.ds(own, 8), :] * u + vel[1, pl.ds(own, 8), :] * v
            total = total + REGULAR * smooth - jnp.exp(mine[:, inner]) * data
        gsum[pl.ds(pl.multiple_of(8 * k, 8), 8), :] = total
        return carry

    lax.fori_loop(0, rows // CB, third, 0)
    sums = jnp.sum(gsum[...].reshape(rows // CB, 8, cols), axis=1)
    cell = lax.broadcasted_iota(jnp.int32, (cols, cols // CB), 0) // CB
    column = lax.broadcasted_iota(jnp.int32, (cols, cols // CB), 1)
    pick = (cell == column).astype(jnp.float32)
    coarse = jnp.dot(
        sums, pick, preferred_element_type=jnp.float32, precision=lax.Precision.HIGHEST
    )
    share = coarse_out.shape[1]
    for i in range(coarse_out.shape[0]):
        coarse_out[i] = coarse[i * share : (i + 1) * share]


SIDES = [(dy, dx) for dy in (-1, 0, 1) for dx in (-1, 0, 1) if (dy, dx) != (0, 0)]


def present(dy, dx):
    y, x = lax.axis_index("ty") + dy, lax.axis_index("tx") + dx
    inside = (y >= 0) & (y < lax.axis_size("ty")) & (x >= 0) & (x < lax.axis_size("tx"))
    return inside, (y, x)


def edge_spots(dy, dx, core, halo):
    north, south, west, east = core
    top, bottom, left, right, corner = halo
    if dx == 0:
        return (north, bottom) if dy == -1 else (south, top)
    if dy == 0:
        return (west, right) if dx == -1 else (east, left)
    src = north if dy == -1 else south
    start = 0 if dx == -1 else src.shape[1] - CH
    k = (0 if dy == 1 else 2) + (0 if dx == 1 else 1)
    return src.at[:, pl.ds(start, CH)], corner.at[k]


def edge_copies(core, halo, send, recv):
    for k, (dy, dx) in enumerate(SIDES):
        src, dst = edge_spots(dy, dx, core, halo)
        there, where = present(dy, dx)
        copy = pltpu.make_async_remote_copy(
            src_ref=src,
            dst_ref=dst,
            send_sem=send.at[k],
            recv_sem=recv.at[k],
            device_id=where,
            device_id_type=pl.DeviceIdType.MESH,
        )
        yield copy, dst, there, present(-dy, -dx)[0]


def start_edges(core, halo, send, recv):
    for copy, dst, there, source in edge_copies(core, halo, send, recv):

        @pl.when(there)
        def _(copy=copy):
            copy.start()

        @pl.when(jnp.logical_not(source))
        def _(dst=dst):
            dst[...] = jnp.zeros(dst.shape, jnp.float32)


def finish_edges(core, halo, send, recv):
    for copy, _, there, source in edge_copies(core, halo, send, recv):

        @pl.when(there)
        def _(copy=copy):
            copy.wait_send()

        @pl.when(source)
        def _(copy=copy):
            copy.wait_recv()


def exchange_kernel(
    packed, north, south, west, east, got, top, bottom, left, right, corner,
    send, recv, edge_send, edge_recv, local,
):
    devices = packed.shape[0]
    nty, ntx = lax.axis_size("ty"), lax.axis_size("tx")
    me = lax.axis_index("ty") * ntx + lax.axis_index("tx")
    barrier = pltpu.get_barrier_semaphore()

    def place(d):
        turn = lax.rem(d + nty // 2, devices)
        y = lax.rem(lax.axis_index("ty") + nty + nty // 2 - lax.rem(turn, nty), nty)
        x = lax.rem(lax.axis_index("tx") + turn // nty, ntx)
        return y * ntx + x, (y, x)

    def greet(d, carry):
        pl.semaphore_signal(
            barrier, inc=1, device_id=place(d)[1], device_id_type=pl.DeviceIdType.MESH
        )
        return carry

    lax.fori_loop(1, devices, greet, 0)
    pl.semaphore_wait(barrier, devices - 1)

    def row_copy(d):
        target, where = place(d)
        return pltpu.make_async_remote_copy(
            src_ref=packed.at[target],
            dst_ref=got.at[me],
            send_sem=send.at[d],
            recv_sem=recv.at[d],
            device_id=where,
            device_id_type=pl.DeviceIdType.MESH,
        )

    def begin(d, carry):
        row_copy(d).start()
        return carry

    lax.fori_loop(1, devices, begin, 0)
    own = pltpu.make_async_copy(packed.at[me], got.at[me], local)
    own.start()
    edges = ((north, south, west, east), (top, bottom, left, right, corner))
    start_edges(*edges, edge_send, edge_recv)
    finish_edges(*edges, edge_send, edge_recv)
    own.wait()

    def finish(d, carry):
        copy = row_copy(d)
        copy.wait_send()
        copy.wait_recv()
        return carry

    lax.fori_loop(1, devices, finish, 0)


def edge_kernel(north, south, west, east, top, bottom, left, right, corner, send, recv):
    barrier = pltpu.get_barrier_semaphore()
    for dy, dx in SIDES:
        there, where = present(dy, dx)

        @pl.when(there)
        def _(where=where):
            pl.semaphore_signal(
                barrier, inc=1, device_id=where, device_id_type=pl.DeviceIdType.MESH
            )

    peers = sum(present(dy, dx)[0].astype(jnp.int32) for dy, dx in SIDES)
    pl.semaphore_wait(barrier, peers)

    edges = ((north, south, west, east), (top, bottom, left, right, corner))
    start_edges(*edges, send, recv)
    finish_edges(*edges, send, recv)


def coarse_kernel(part, out, held, send, recv):
    count = part.shape[0]
    ty, me = lax.axis_index("ty"), lax.axis_index("tx")
    barrier = pltpu.get_barrier_semaphore()
    for d in range(1, count):
        pl.semaphore_signal(
            barrier,
            inc=1,
            device_id=(ty, lax.rem(me + d, count)),
            device_id_type=pl.DeviceIdType.MESH,
        )
    pl.semaphore_wait(barrier, count - 1)
    copies = []
    for d in range(1, count):
        target = lax.rem(me + d, count)
        copy = pltpu.make_async_remote_copy(
            src_ref=part.at[target],
            dst_ref=held.at[me],
            send_sem=send.at[d],
            recv_sem=recv.at[d],
            device_id=(ty, target),
            device_id_type=pl.DeviceIdType.MESH,
        )
        copy.start()
        copies.append(copy)
    held[me] = part[me]
    for copy in copies:
        copy.wait_send()
        copy.wait_recv()
    width = part.shape[2]
    for i in range(count):
        out[:, i * width : (i + 1) * width] = held[i]


VMEM = pl.BlockSpec(memory_space=pltpu.VMEM)
SMEM = pl.BlockSpec(memory_space=pltpu.SMEM)
ANY = pl.BlockSpec(memory_space=pl.ANY)


def shards(track_rows, track_tile, track_slot, velocity, viscosity, log_friction):
    rows, cols = viscosity.shape
    tiles_x = lax.axis_size("tx")
    devices = lax.axis_size("ty") * tiles_x
    rows_dev, _, seg = track_rows.shape
    cap = max(2, 2 * rows_dev // devices)
    params = pltpu.CompilerParams(vmem_limit_bytes=VMEM_LIMIT)
    f32 = jnp.float32
    block = track_rows.reshape(rows_dev, 2, 2, 128).transpose(0, 2, 1, 3).reshape(rows_dev, 4, 128)
    edge_shapes = [
        jax.ShapeDtypeStruct(shape, f32) for shape in ((RH, cols),) * 2 + ((RH, rows),) * 2
    ]
    halo_shapes = edge_shapes + [jax.ShapeDtypeStruct((4, RH, CH), f32)]
    packed, *eq_edges = pl.pallas_call(
        functools.partial(pack_kernel, cap),
        out_shape=[jax.ShapeDtypeStruct((devices, cap + 1, 4, 128), f32)] + edge_shapes,
        in_specs=[SMEM, SMEM, VMEM, ANY, ANY],
        out_specs=[VMEM] * 5,
        scratch_shapes=[
            pltpu.SMEM((devices,), jnp.int32),
            pltpu.VMEM((4, RH, cols), f32),
            pltpu.VMEM((4, rows, CH), f32),
            pltpu.SemaphoreType.DMA((8,)),
        ],
        compiler_params=params,
        name="pack",
    )(track_tile[:, 0], track_slot, block, viscosity, log_friction)

    def remote(number):
        return pltpu.CompilerParams(
            collective_id=number, has_side_effects=True, vmem_limit_bytes=VMEM_LIMIT
        )

    got, *eq_halo = pl.pallas_call(
        exchange_kernel,
        out_shape=[jax.ShapeDtypeStruct(packed.shape, f32)] + halo_shapes,
        in_specs=[ANY] + [VMEM] * 4,
        out_specs=[ANY] + [VMEM] * 5,
        scratch_shapes=[
            pltpu.SemaphoreType.DMA((devices,)),
            pltpu.SemaphoreType.DMA((devices,)),
            pltpu.SemaphoreType.DMA((8,)),
            pltpu.SemaphoreType.DMA((8,)),
            pltpu.SemaphoreType.DMA,
        ],
        compiler_params=remote(0),
        name="exchange",
    )(packed, *eq_edges)
    meta = got[:, cap, 0, :].astype(jnp.int32).reshape(devices * 128)
    forcing, *f_edges = pl.pallas_call(
        functools.partial(scatter_kernel, cap, cols // seg),
        out_shape=[jax.ShapeDtypeStruct((2, rows, cols), f32)] + edge_shapes,
        in_specs=[SMEM, VMEM],
        out_specs=[VMEM] * 5,
        scratch_shapes=[pltpu.VMEM((2, rows, cols), f32)],
        compiler_params=params,
        name="scatter",
    )(meta, got)
    f_halo = pl.pallas_call(
        edge_kernel,
        out_shape=halo_shapes,
        in_specs=[VMEM] * 4,
        out_specs=[VMEM] * 5,
        scratch_shapes=[pltpu.SemaphoreType.DMA((8,)), pltpu.SemaphoreType.DMA((8,))],
        compiler_params=remote(1),
        name="edges",
    )(*f_edges)
    coarse_rows = rows // CB
    big = (rows + 2 * R0, cols + 2 * CH)
    adjoint, coarse = pl.pallas_call(
        stencil_kernel,
        out_shape=(
            jax.ShapeDtypeStruct((2, rows, cols), f32),
            jax.ShapeDtypeStruct((tiles_x, coarse_rows // tiles_x, cols // CB), f32),
        ),
        in_specs=[ANY] + [VMEM] * 5 + [ANY] * 2 + [VMEM] * 5 + [ANY],
        out_specs=(VMEM, VMEM),
        scratch_shapes=[
            pltpu.VMEM((2,) + big, f32),
            pltpu.VMEM(big, f32),
            pltpu.VMEM(big, f32),
            pltpu.VMEM((2,) + big, f32),
            pltpu.VMEM((2,) + big, f32),
            pltpu.VMEM((2,) + big, f32),
            pltpu.VMEM((2, rows, cols), f32),
            pltpu.VMEM((coarse_rows * 8, cols), f32),
            pltpu.SemaphoreType.DMA((5,)),
        ],
        compiler_params=params,
        name="stencil",
    )(forcing, *f_halo, viscosity, log_friction, *eq_halo, velocity)
    grad = pl.pallas_call(
        coarse_kernel,
        out_shape=jax.ShapeDtypeStruct((coarse_rows // tiles_x, cols // CB * tiles_x), f32),
        in_specs=[VMEM],
        out_specs=VMEM,
        scratch_shapes=[
            pltpu.VMEM(coarse.shape, f32),
            pltpu.SemaphoreType.DMA((tiles_x,)),
            pltpu.SemaphoreType.DMA((tiles_x,)),
        ],
        compiler_params=remote(2),
        name="coarse",
    )(coarse)
    return adjoint, grad


def solution(mesh):
    return jax.shard_map(
        shards,
        mesh=mesh,
        in_specs=(
            P(("ty", "tx"), None, None),
            P(("ty", "tx"), None),
            P(("ty", "tx")),
            P(None, "ty", "tx"),
            P("ty", "tx"),
            P("ty", "tx"),
        ),
        out_specs=(P(None, "ty", "tx"), P(("ty", "tx"), None)),
        check_vma=False,
    )
```

```python
import functools

import jax
import jax.numpy as jnp
from jax import lax
from jax.experimental import pallas as pl
from jax.experimental.pallas import tpu as pltpu
from jax.sharding import PartitionSpec as P

CB = 16
OMEGA = 0.8
REGULAR = 0.1
RH = 8
CH = 128
R0 = 16
VMEM_LIMIT = 56 * 1024 * 1024


def compact(fields):
    half = RH // 2
    north = [top[:half] for top, _, _, _ in fields]
    south = [bottom[half:] for _, bottom, _, _ in fields]
    west = [left.T[:half] for _, _, left, _ in fields]
    east = [right.T[CH - half :] for _, _, _, right in fields]
    return [jnp.concatenate(parts, axis=0) for parts in (north, south, west, east)]


def pack_kernel(
    cap, tile_ref, slot_ref, rows_ref, eta_in, q_in,
    out_ref, north, south, west, east,
    count, row_edges, col_edges, sems,
):
    devices = out_ref.shape[0]
    rows, cols = eta_in.shape
    copies = []
    for i, x in enumerate((eta_in, q_in)):
        spots = (
            (x.at[pl.ds(0, RH), :], row_edges.at[2 * i]),
            (x.at[pl.ds(rows - RH, RH), :], row_edges.at[2 * i + 1]),
            (x.at[:, pl.ds(0, CH)], col_edges.at[2 * i]),
            (x.at[:, pl.ds(cols - CH, CH)], col_edges.at[2 * i + 1]),
        )
        for j, (src, dst) in enumerate(spots):
            copies.append(pltpu.make_async_copy(src, dst, sems.at[4 * i + j]))
    for copy in copies:
        copy.start()
    lanes = lax.broadcasted_iota(jnp.int32, (4, 128), 1)

    def clear(d, carry):
        count[d] = 0
        out_ref[d, cap] = jnp.zeros((4, 128), jnp.float32)
        return carry

    lax.fori_loop(0, devices, clear, 0)

    def place(i, carry):
        t = tile_ref[i]
        r = count[t]
        count[t] = r + 1
        out_ref[t, r] = rows_ref[i]
        slot = slot_ref[i].astype(jnp.float32)
        filled = (r + 1).astype(jnp.float32)
        head = out_ref[t, cap]
        out_ref[t, cap] = jnp.where(lanes == r, slot, jnp.where(lanes == cap, filled, head))
        return carry

    lax.fori_loop(0, rows_ref.shape[0], place, 0, unroll=4)
    for copy in copies:
        copy.wait()
    fields = [
        (row_edges[2 * i], row_edges[2 * i + 1], col_edges[2 * i], col_edges[2 * i + 1])
        for i in range(2)
    ]
    for ref, value in zip((north, south, west, east), compact(fields)):
        ref[...] = value


def scatter_kernel(cap, segs, meta_ref, got_ref, out_ref, north, south, west, east, second):
    out_ref[...] = jnp.zeros_like(out_ref)
    lanes = lax.broadcasted_iota(jnp.int32, (8, 128), 0)

    second[...] = jnp.zeros_like(second)
    step = 8 if cap % 8 == 0 else 2 if cap % 2 == 0 else 1
    shift = segs.bit_length() - 1 if segs & (segs - 1) == 0 else None

    def source(s, carry):
        filled = meta_ref[s * 128 + cap]

        def add(k, inner):
            spots, news = [], []
            for i in range(step):
                r = k * step + i
                slot = meta_ref[s * 128 + r]
                y = slot // segs if shift is None else slot >> shift
                x = pl.multiple_of((slot - y * segs) * 256, 256)
                base = pl.multiple_of((y >> 3) * 8, 8)
                chosen = lanes == jnp.where(r < filled, y - base, -1)
                spots.append(
                    [(c, pl.ds(base, 8), pl.ds(x + 128 * h, 128)) for h in range(2) for c in range(2)]
                )
                row = [got_ref[s, r, pl.ds(j, 1), :] for j in range(4)]
                news.append([jnp.where(chosen, part, 0.0) for part in row])
            for i in range(0, step, 2):
                pairs = list(zip((out_ref, second), spots[i : i + 2], news[i : i + 2]))
                sums = [
                    [ref[spot] + new for spot, new in zip(where, what)] for ref, where, what in pairs
                ]
                for (ref, where, _), values in zip(pairs, sums):
                    for spot, value in zip(where, values):
                        ref[spot] = value
            return inner

        return lax.fori_loop(0, lax.div(filled + step - 1, step), add, carry)

    lax.fori_loop(0, got_ref.shape[0], source, 0)
    out_ref[...] += second[...]
    _, rows, cols = out_ref.shape
    fields = [
        (
            out_ref[c, :RH, :],
            out_ref[c, rows - RH :, :],
            out_ref[c, :, :CH],
            out_ref[c, :, cols - CH :],
        )
        for c in range(2)
    ]
    for ref, value in zip((north, south, west, east), compact(fields)):
        ref[...] = value


def stencil_kernel(
    f_in, ft, fb, fl, fr, fc, eta_in, q_in, et, eb, el, er, ec, vel_in,
    adj_out, coarse_out,
    f, eta, q, a0, a1, inv, vel, gsum, sems,
):
    _, rows, cols = f_in.shape
    width = cols + 2 * CH
    ty, tx = lax.axis_index("ty"), lax.axis_index("tx")
    mid = (pl.ds(R0, rows), pl.ds(CH, cols))
    moves = [(eta_in, eta.at[mid]), (q_in, q.at[mid])]
    for c in range(2):
        moves.append((f_in.at[c], f.at[(c,) + mid]))
    n_second = len(moves)
    moves.append((vel_in, vel))
    copies = [pltpu.make_async_copy(a, b, sems.at[i]) for i, (a, b) in enumerate(moves)]
    for copy in copies:
        copy.start()
    half = RH // 2
    above, below = slice(R0 - RH, R0), slice(R0 + rows, R0 + rows + RH)
    core, first, last = slice(CH, CH + cols), slice(0, CH), slice(CH + cols, width)

    def spread(i, edges, put):
        top, bottom, left, right, corner = edges
        own = slice(half * i, half * i + half)
        for span, x, block in (
            (above, core, top[own, :]),
            (below, core, bottom[own, :]),
            (above, first, corner[0, own, :]),
            (above, last, corner[1, own, :]),
            (below, first, corner[2, own, :]),
            (below, last, corner[3, own, :]),
        ):
            rest = jnp.zeros_like(block)
            parts = [rest, block] if span == above else [block, rest]
            put(span, x, jnp.concatenate(parts, axis=0))
        rest = jnp.zeros((CH - half, rows), jnp.float32)
        tall = slice(R0, R0 + rows)
        put(tall, first, jnp.concatenate([rest, left[own, :]], axis=0).T)
        put(tall, last, jnp.concatenate([right[own, :], rest], axis=0).T)

    def put_into(ref, *lead):
        def put(y, x, value):
            ref[lead + (y, x)] = value

        return put

    for i in range(2):
        spread(i, (et, eb, el, er, ec), put_into((eta, q)[i]))
        spread(i, (ft, fb, fl, fr, fc), put_into(f, i))
    for copy in copies[:n_second]:
        copy.wait()

    def window(ref, start, *lead):
        return ref[lead + (pl.ds(start - 8, 24), slice(None))]

    def shifts(w):
        return w[9:17], w[7:15]

    def to_left(x):
        return pltpu.roll(x, width - 1, 1)

    def to_right(x):
        return pltpu.roll(x, 1, 1)

    def prepare(k, carry):
        start = pl.multiple_of(8 * k, 8)
        here = pl.ds(start, 8)
        w = window(eta, start)
        mine = w[8:16]
        nxt, prv = shifts(w)
        y_sum = nxt + prv
        x_sum = to_left(mine) + to_right(mine)
        base = 5.0 * mine + jnp.exp(q[here, :])
        inv_u = OMEGA / (base + 2.0 * x_sum + 0.5 * y_sum)
        inv_v = OMEGA / (base + 2.0 * y_sum + 0.5 * x_sum)
        inv[0, here, :] = inv_u
        inv[1, here, :] = inv_v
        a0[0, here, :] = inv_u * f[0, here, :]
        a0[1, here, :] = inv_v * f[1, here, :]
        return carry

    chunks = (rows + 2 * RH) // 8
    lax.fori_loop(1, 1 + chunks, prepare, 0)

    def sweep(src, start):
        here = pl.ds(start, 8)
        e = window(eta, start)
        u, v = window(src, start, 0), window(src, start, 1)
        gu, gv = e * u, e * v
        em, um, vm = e[8:16], u[8:16], v[8:16]
        gum, gvm = gu[8:16], gv[8:16]
        un, us = shifts(u)
        vn, vs = shifts(v)
        gun, gus = shifts(gu)
        gvn, gvs = shifts(gv)
        du, dv = 0.75 * (un - us), 0.75 * (vn - vs)
        u2, v2 = 2.0 * um, 0.5 * vm
        su = f[0, here, :] + em * (to_left(u2 + dv) + to_right(u2 - dv) + 0.5 * (un + us))
        su = su + 2.0 * (to_left(gum) + to_right(gum)) + 0.5 * (gun + gus)
        sv = f[1, here, :] + em * (to_left(v2 + du) + to_right(v2 - du) + 2.0 * (vn + vs))
        sv = sv + 0.5 * (to_left(gvm) + to_right(gvm)) + 2.0 * (gvn + gvs)
        keep = 1.0 - OMEGA
        return keep * um + inv[0, here, :] * su, keep * vm + inv[1, here, :] * sv

    def second(k, carry):
        start = pl.multiple_of(8 * k, 8)
        u, v = sweep(a0, start)
        a1[0, pl.ds(start, 8), :] = u
        a1[1, pl.ds(start, 8), :] = v
        return carry

    lax.fori_loop(1, 1 + chunks, second, 0)

    @pl.when(ty == 0)
    def _():
        a1[:, R0 - RH : R0, :] = jnp.zeros((2, RH, width), jnp.float32)

    @pl.when(ty == lax.axis_size("ty") - 1)
    def _():
        a1[:, R0 + rows : R0 + rows + RH, :] = jnp.zeros((2, RH, width), jnp.float32)

    @pl.when(tx == 0)
    def _():
        a1[:, :, :CH] = jnp.zeros((2, a1.shape[1], CH), jnp.float32)

    @pl.when(tx == lax.axis_size("tx") - 1)
    def _():
        a1[:, :, CH + cols :] = jnp.zeros((2, a1.shape[1], CH), jnp.float32)

    copies[-1].wait()
    inner = slice(CH, CH + cols)

    def third(k, carry):
        total = jnp.zeros((8, cols), jnp.float32)
        for half in range(CB // 8):
            own = pl.multiple_of(CB * k + 8 * half, 8)
            start = pl.multiple_of(own + R0, 8)
            u, v = sweep(a1, start)
            u, v = u[:, inner], v[:, inner]
            adj_out[0, pl.ds(own, 8), :] = u
            adj_out[1, pl.ds(own, 8), :] = v
            w = window(q, start)
            nxt, prv = shifts(w)
            mine = w[8:16]
            smooth = (4.0 * mine - (to_left(mine) + to_right(mine) + nxt + prv))[:, inner]
            data = vel[0, pl.ds(own, 8), :] * u + vel[1, pl.ds(own, 8), :] * v
            total = total + REGULAR * smooth - jnp.exp(mine[:, inner]) * data
        gsum[pl.ds(pl.multiple_of(8 * k, 8), 8), :] = total
        return carry

    lax.fori_loop(0, rows // CB, third, 0)
    sums = jnp.sum(gsum[...].reshape(rows // CB, 8, cols), axis=1)
    cell = lax.broadcasted_iota(jnp.int32, (cols, cols // CB), 0) // CB
    column = lax.broadcasted_iota(jnp.int32, (cols, cols // CB), 1)
    pick = (cell == column).astype(jnp.float32)
    coarse = jnp.dot(
        sums, pick, preferred_element_type=jnp.float32, precision=lax.Precision.HIGHEST
    )
    share = coarse_out.shape[1]
    for i in range(coarse_out.shape[0]):
        coarse_out[i] = coarse[i * share : (i + 1) * share]


SIDES = [(dy, dx) for dy in (-1, 0, 1) for dx in (-1, 0, 1) if (dy, dx) != (0, 0)]


def present(dy, dx):
    y, x = lax.axis_index("ty") + dy, lax.axis_index("tx") + dx
    inside = (y >= 0) & (y < lax.axis_size("ty")) & (x >= 0) & (x < lax.axis_size("tx"))
    return inside, (y, x)


def edge_spots(dy, dx, core, halo):
    north, south, west, east = core
    top, bottom, left, right, corner = halo
    if dx == 0:
        return (north, bottom) if dy == -1 else (south, top)
    if dy == 0:
        return (west, right) if dx == -1 else (east, left)
    src = north if dy == -1 else south
    start = 0 if dx == -1 else src.shape[1] - CH
    k = (0 if dy == 1 else 2) + (0 if dx == 1 else 1)
    return src.at[:, pl.ds(start, CH)], corner.at[k]


def edge_copies(core, halo, send, recv):
    for k, (dy, dx) in enumerate(SIDES):
        src, dst = edge_spots(dy, dx, core, halo)
        there, where = present(dy, dx)
        copy = pltpu.make_async_remote_copy(
            src_ref=src,
            dst_ref=dst,
            send_sem=send.at[k],
            recv_sem=recv.at[k],
            device_id=where,
            device_id_type=pl.DeviceIdType.MESH,
        )
        yield copy, dst, there, present(-dy, -dx)[0]


def start_edges(core, halo, send, recv):
    for copy, dst, there, source in edge_copies(core, halo, send, recv):

        @pl.when(there)
        def _(copy=copy):
            copy.start()

        @pl.when(jnp.logical_not(source))
        def _(dst=dst):
            dst[...] = jnp.zeros(dst.shape, jnp.float32)


def finish_edges(core, halo, send, recv):
    for copy, _, there, source in edge_copies(core, halo, send, recv):

        @pl.when(there)
        def _(copy=copy):
            copy.wait_send()

        @pl.when(source)
        def _(copy=copy):
            copy.wait_recv()


def exchange_kernel(
    packed, north, south, west, east, got, top, bottom, left, right, corner,
    send, recv, edge_send, edge_recv, local,
):
    devices = packed.shape[0]
    nty, ntx = lax.axis_size("ty"), lax.axis_size("tx")
    me = lax.axis_index("ty") * ntx + lax.axis_index("tx")
    barrier = pltpu.get_barrier_semaphore()

    def place(d):
        turn = lax.rem(d + nty // 2, devices)
        y = lax.rem(lax.axis_index("ty") + nty + nty // 2 - lax.rem(turn, nty), nty)
        x = lax.rem(lax.axis_index("tx") + turn // nty, ntx)
        return y * ntx + x, (y, x)

    def greet(d, carry):
        pl.semaphore_signal(
            barrier, inc=1, device_id=place(d)[1], device_id_type=pl.DeviceIdType.MESH
        )
        return carry

    lax.fori_loop(1, devices, greet, 0)
    pl.semaphore_wait(barrier, devices - 1)

    def row_copy(d):
        target, where = place(d)
        return pltpu.make_async_remote_copy(
            src_ref=packed.at[target],
            dst_ref=got.at[me],
            send_sem=send.at[d],
            recv_sem=recv.at[d],
            device_id=where,
            device_id_type=pl.DeviceIdType.MESH,
        )

    def begin(d, carry):
        row_copy(d).start()
        return carry

    lax.fori_loop(1, devices, begin, 0)
    own = pltpu.make_async_copy(packed.at[me], got.at[me], local)
    own.start()
    edges = ((north, south, west, east), (top, bottom, left, right, corner))
    start_edges(*edges, edge_send, edge_recv)
    finish_edges(*edges, edge_send, edge_recv)
    own.wait()

    def finish(d, carry):
        copy = row_copy(d)
        copy.wait_send()
        copy.wait_recv()
        return carry

    lax.fori_loop(1, devices, finish, 0)


def edge_kernel(north, south, west, east, top, bottom, left, right, corner, send, recv):
    barrier = pltpu.get_barrier_semaphore()
    for dy, dx in SIDES:
        there, where = present(dy, dx)

        @pl.when(there)
        def _(where=where):
            pl.semaphore_signal(
                barrier, inc=1, device_id=where, device_id_type=pl.DeviceIdType.MESH
            )

    peers = sum(present(dy, dx)[0].astype(jnp.int32) for dy, dx in SIDES)
    pl.semaphore_wait(barrier, peers)

    edges = ((north, south, west, east), (top, bottom, left, right, corner))
    start_edges(*edges, send, recv)
    finish_edges(*edges, send, recv)


def coarse_kernel(part, out, held, send, recv):
    count = part.shape[0]
    ty, me = lax.axis_index("ty"), lax.axis_index("tx")
    barrier = pltpu.get_barrier_semaphore()
    for d in range(1, count):
        pl.semaphore_signal(
            barrier,
            inc=1,
            device_id=(ty, lax.rem(me + d, count)),
            device_id_type=pl.DeviceIdType.MESH,
        )
    pl.semaphore_wait(barrier, count - 1)
    copies = []
    for d in range(1, count):
        target = lax.rem(me + d, count)
        copy = pltpu.make_async_remote_copy(
            src_ref=part.at[target],
            dst_ref=held.at[me],
            send_sem=send.at[d],
            recv_sem=recv.at[d],
            device_id=(ty, target),
            device_id_type=pl.DeviceIdType.MESH,
        )
        copy.start()
        copies.append(copy)
    held[me] = part[me]
    for copy in copies:
        copy.wait_send()
        copy.wait_recv()
    width = part.shape[2]
    for i in range(count):
        out[:, i * width : (i + 1) * width] = held[i]


VMEM = pl.BlockSpec(memory_space=pltpu.VMEM)
SMEM = pl.BlockSpec(memory_space=pltpu.SMEM)
ANY = pl.BlockSpec(memory_space=pl.ANY)


def shards(track_rows, track_tile, track_slot, velocity, viscosity, log_friction):
    rows, cols = viscosity.shape
    tiles_x = lax.axis_size("tx")
    devices = lax.axis_size("ty") * tiles_x
    rows_dev, _, seg = track_rows.shape
    cap = max(2, 2 * rows_dev // devices)
    params = pltpu.CompilerParams(vmem_limit_bytes=VMEM_LIMIT)
    f32 = jnp.float32
    block = track_rows.reshape(rows_dev, 2, 2, 128).transpose(0, 2, 1, 3).reshape(rows_dev, 4, 128)
    edge_shapes = [
        jax.ShapeDtypeStruct(shape, f32) for shape in ((RH, cols),) * 2 + ((RH, rows),) * 2
    ]
    halo_shapes = edge_shapes + [jax.ShapeDtypeStruct((4, RH, CH), f32)]
    packed, *eq_edges = pl.pallas_call(
        functools.partial(pack_kernel, cap),
        out_shape=[jax.ShapeDtypeStruct((devices, cap + 1, 4, 128), f32)] + edge_shapes,
        in_specs=[SMEM, SMEM, VMEM, ANY, ANY],
        out_specs=[VMEM] * 5,
        scratch_shapes=[
            pltpu.SMEM((devices,), jnp.int32),
            pltpu.VMEM((4, RH, cols), f32),
            pltpu.VMEM((4, rows, CH), f32),
            pltpu.SemaphoreType.DMA((8,)),
        ],
        compiler_params=params,
        name="pack",
    )(track_tile[:, 0], track_slot, block, viscosity, log_friction)

    def remote(number):
        return pltpu.CompilerParams(
            collective_id=number, has_side_effects=True, vmem_limit_bytes=VMEM_LIMIT
        )

    got, *eq_halo = pl.pallas_call(
        exchange_kernel,
        out_shape=[jax.ShapeDtypeStruct(packed.shape, f32)] + halo_shapes,
        in_specs=[ANY] + [VMEM] * 4,
        out_specs=[ANY] + [VMEM] * 5,
        scratch_shapes=[
            pltpu.SemaphoreType.DMA((devices,)),
            pltpu.SemaphoreType.DMA((devices,)),
            pltpu.SemaphoreType.DMA((8,)),
            pltpu.SemaphoreType.DMA((8,)),
            pltpu.SemaphoreType.DMA,
        ],
        compiler_params=remote(0),
        name="exchange",
    )(packed, *eq_edges)
    meta = got[:, cap, 0, :].astype(jnp.int32).reshape(devices * 128)
    forcing, *f_edges = pl.pallas_call(
        functools.partial(scatter_kernel, cap, cols // seg),
        out_shape=[jax.ShapeDtypeStruct((2, rows, cols), f32)] + edge_shapes,
        in_specs=[SMEM, VMEM],
        out_specs=[VMEM] * 5,
        scratch_shapes=[pltpu.VMEM((2, rows, cols), f32)],
        compiler_params=params,
        name="scatter",
    )(meta, got)
    f_halo = pl.pallas_call(
        edge_kernel,
        out_shape=halo_shapes,
        in_specs=[VMEM] * 4,
        out_specs=[VMEM] * 5,
        scratch_shapes=[pltpu.SemaphoreType.DMA((8,)), pltpu.SemaphoreType.DMA((8,))],
        compiler_params=remote(1),
        name="edges",
    )(*f_edges)
    coarse_rows = rows // CB
    big = (rows + 2 * R0, cols + 2 * CH)
    adjoint, coarse = pl.pallas_call(
        stencil_kernel,
        out_shape=(
            jax.ShapeDtypeStruct((2, rows, cols), f32),
            jax.ShapeDtypeStruct((tiles_x, coarse_rows // tiles_x, cols // CB), f32),
        ),
        in_specs=[ANY] + [VMEM] * 5 + [ANY] * 2 + [VMEM] * 5 + [ANY],
        out_specs=(VMEM, VMEM),
        scratch_shapes=[
            pltpu.VMEM((2,) + big, f32),
            pltpu.VMEM(big, f32),
            pltpu.VMEM(big, f32),
            pltpu.VMEM((2,) + big, f32),
            pltpu.VMEM((2,) + big, f32),
            pltpu.VMEM((2,) + big, f32),
            pltpu.VMEM((2, rows, cols), f32),
            pltpu.VMEM((coarse_rows * 8, cols), f32),
            pltpu.SemaphoreType.DMA((5,)),
        ],
        compiler_params=params,
        name="stencil",
    )(forcing, *f_halo, viscosity, log_friction, *eq_halo, velocity)
    grad = pl.pallas_call(
        coarse_kernel,
        out_shape=jax.ShapeDtypeStruct((coarse_rows // tiles_x, cols // CB * tiles_x), f32),
        in_specs=[VMEM],
        out_specs=VMEM,
        scratch_shapes=[
            pltpu.VMEM(coarse.shape, f32),
            pltpu.SemaphoreType.DMA((tiles_x,)),
            pltpu.SemaphoreType.DMA((tiles_x,)),
        ],
        compiler_params=remote(2),
        name="coarse",
    )(coarse)
    return adjoint, grad


def solution(mesh):
    return jax.shard_map(
        shards,
        mesh=mesh,
        in_specs=(
            P(("ty", "tx"), None, None),
            P(("ty", "tx"), None),
            P(("ty", "tx")),
            P(None, "ty", "tx"),
            P("ty", "tx"),
            P("ty", "tx"),
        ),
        out_specs=(P(None, "ty", "tx"), P(("ty", "tx"), None)),
        check_vma=False,
    )
```
